256 devices in a mesh: pair: 32 (over x, y, core), virt: 8 (over z).
Axes of the slice: x: 4, y: 4, z: 8, core: 2. Of those that a mesh axis runs over, the one named last changes fastest.
Arguments:
- amps: float32 [8, 2048, 2048], P(None, 'pair', 'virt'), may hold values from -6 to 6
- ints: float32 [8, 2048, 2048], P(None, 'pair', 'virt'), may hold values from -0.125 to 0.125
- panel_of: int32 [32], replicated, may hold values from 0 to 31, each once
- e_occ: float32 [8], replicated, may hold values from -2 to -0.5
- e_vir: float32 [2048], replicated, may hold values from 0.2 to 3
Outputs:
- cycle_update: float32 [8, 8, 2048, 2048], P('virt', None, 'pair')
The draws below stay inside these ranges and needn't reach their ends.
Inputs may be any that keep to these rules, and one draw needn't show every extreme that they name: panel_of holds each of 0 to 31 once.
All inputs are finite; a program needn't handle non-finite values.
Results may differ from the reference program's by a relative error of at most 0.00007.
Values sent between devices are 32-bit elements; how exact they have to be, the bound alone decides.
No kernel may reach another device: no remote copies, remote signals or barrier semaphores. Data moves between devices by JAX's collectives and lax.ppermute only.
A program may use at most 192 MiB of HBM per device.

```python
import jax
import jax.numpy as jnp
from jax import lax

V = 2048
NOCC = 8
PANEL = 64
N_PAIR = 32


def shard_levels(stream_key, shape, cuts, least, top_value):
    def one(position, parts):
        draws = jax.random.uniform(jax.random.fold_in(jax.random.fold_in(stream_key, 6), position), (parts,), jnp.float32, least / len(cuts), top_value / len(cuts))
        return jnp.repeat(jnp.exp(draws), shape[position] // parts).reshape((-1,) + (1,) * (len(shape) - position - 1))

    gain = one(*cuts[0])
    for cut in cuts[1:]:
        gain = gain * one(*cut)
    return gain


def scatter_about(key, dims, scale, reach, cuts=(), held_as=jnp.bfloat16):
    drawn = jax.random.normal(key, dims, jnp.float32) * scale
    if len(cuts) > 0:
        drawn = shard_levels(key, dims, cuts, -0.22, 0.18) * drawn
    return jnp.clip(drawn, min=-reach, max=reach).astype(held_as)


def setup_inputs(seed: int = 0) -> dict:
    seeds = jax.random.split(jax.random.key(seed), 6)
    amps = scatter_about(seeds[0], (NOCC, V, V), 1.0, 6.0, ((1, 32), (2, 8)), jnp.float32)
    ints = scatter_about(seeds[1], (NOCC, V, V), V ** -0.5, 0.125, ((1, 32), (2, 8)), jnp.float32)
    panel_of = jax.random.permutation(seeds[2], N_PAIR).astype(jnp.int32)
    e_occ = jnp.clip(jax.random.uniform(seeds[3], (NOCC,), jnp.float32, -2.0, -0.5), -2.0, -0.5)
    e_vir = jnp.clip(jax.random.uniform(seeds[4], (V,), jnp.float32, 0.2, 3.0), 0.2, 3.0)
    return {"amps": amps, "ints": ints, "panel_of": panel_of, "e_occ": e_occ, "e_vir": e_vir}


def reference(amps, ints, panel_of, e_occ, e_vir):
    rows = jnp.arange(V, dtype=jnp.int32)
    dest = panel_of[rows // PANEL] * PANEL + rows % PANEL
    amp_true = jnp.zeros((NOCC, V, V), jnp.float32).at[:, dest, :].set(amps)

    def one_row(amp_one):
        return jnp.einsum("ac,jbc->jba", amp_one, ints, precision=lax.Precision.HIGHEST, preferred_element_type=jnp.float32)

    cycle = lax.map(one_row, amp_true)

    def finish(index):
        direct = cycle[index]
        mirrored = cycle[:, index]
        denom = e_occ[index] + e_occ[:, None, None] - e_vir[None, :, None] - e_vir[None, None, :]
        return (direct - mirrored) / denom

    return lax.map(finish, jnp.arange(NOCC, dtype=jnp.int32))
```

```python
import functools

import jax
import jax.numpy as jnp
from jax import lax
from jax.experimental import pallas as pl
from jax.experimental.pallas import tpu as pltpu
from jax.sharding import PartitionSpec as P

CHUNKS = 4
RING = 8
NT = (((1,), (1,)), ((), ()))
SMEM = pl.BlockSpec(memory_space=pltpu.SMEM)
HBM = pl.BlockSpec(memory_space=pltpu.HBM)
VMEM = pl.BlockSpec(memory_space=pltpu.VMEM)


def split(x):
    high = x.astype(jnp.bfloat16)
    return high, (x - high.astype(jnp.float32)).astype(jnp.bfloat16)


def product_kernel(dims, pos, panel_of, amp_hbm, *refs):
    count, rows, occ, panel, width = dims
    ints = refs[: 2 * RING]
    out_hbm, amp, a_hi, a_lo, i_hi, i_lo, total, packed, sem, out_sem = refs[2 * RING :]
    v = pos[0]
    half = occ // 2

    def start(q, carry):
        pltpu.make_async_copy(amp_hbm.at[q], amp.at[panel_of[q]], sem).start()
        return carry

    lax.fori_loop(0, count, start, 0)
    for s in range(RING):
        for part in range(2):
            block = ints[2 * s + part]
            hi, lo = split(block[...].reshape(half * panel, width))
            at = slice(part * half * panel, (part + 1) * half * panel)
            i_hi[at, s * width : (s + 1) * width] = hi
            i_lo[at, s * width : (s + 1) * width] = lo
    pltpu.make_async_copy(amp_hbm, amp, sem).wait()
    for s in range(RING):
        source = lax.rem(v - s + RING, RING)
        hi, lo = split(amp[:, source].reshape(count * rows, width))
        a_hi[:, s * width : (s + 1) * width] = hi
        a_lo[:, s * width : (s + 1) * width] = lo
    dot = functools.partial(lax.dot_general, dimension_numbers=NT, preferred_element_type=jnp.float32)
    step = count * rows // 2
    for m in range(2):
        at = slice(m * step, (m + 1) * step)
        total[at] = dot(a_hi[at], i_lo[...]) + dot(a_lo[at], i_hi[...]) + dot(a_hi[at], i_hi[...])
    lane = lax.broadcasted_iota(jnp.int32, (step, 2 * panel), 1)
    for p in range(occ // 2):
        cols = slice(2 * panel * p, 2 * panel * (p + 1))
        top, low = total[:step, cols], total[step:, cols]
        packed[2 * p] = jnp.where(lane < panel, top, pltpu.roll(low, panel, 1))
        packed[2 * p + 1] = jnp.where(lane < panel, pltpu.roll(top, panel, 1), low)
    copy = pltpu.make_async_copy(packed, out_hbm, out_sem)
    copy.start()
    copy.wait()


def finish_kernel(dims, pos, e_occ, e_b, e_vir, *refs):
    rows, occ, panel, virtuals = dims
    direct, mirror = refs[:CHUNKS], refs[CHUNKS : 2 * CHUNKS]
    out_hbm, dir_v, mir_v, out_v, in_sem, out_sem = refs[2 * CHUNKS :]
    v = pos[0]
    loads = [
        [pltpu.make_async_copy(direct[k].at[j], dir_v.at[j, k], in_sem.at[j, k]) for k in range(CHUNKS)]
        + [pltpu.make_async_copy(mirror[k].at[j], mir_v.at[j, k], in_sem.at[j, CHUNKS + k]) for k in range(CHUNKS)]
        for j in range(occ)
    ]
    for j in range(occ):
        for copy in loads[j]:
            copy.start()
    lanes = 2 * panel
    for j in range(occ):
        for copy in loads[j]:
            copy.wait()
        base = (e_occ[v] + e_occ[j]) - e_b[...]
        for t in range(virtuals // 2 // lanes):
            parts = []
            for m in (2 * t, 2 * t + 1):
                for k in range(CHUNKS):
                    at = slice(m * rows, (m + 1) * rows)
                    parts.append(dir_v[j, k, at, :] - mir_v[j, k, at, :])
            block = jnp.concatenate(parts, axis=0).T
            for h in range(2):
                cols = slice(h * virtuals // 2 + t * lanes, h * virtuals // 2 + (t + 1) * lanes)
                out_v[j, :, cols] = block[h * panel : (h + 1) * panel, :] / (base - e_vir[:, cols])
        pltpu.make_async_copy(out_v.at[j], out_hbm.at[j], out_sem.at[j]).start()
    for j in range(occ):
        pltpu.make_async_copy(out_v.at[j], out_hbm.at[j], out_sem.at[j]).wait()


def body(amps, ints, panel_of, e_occ, e_vir):
    occ, panel, width = amps.shape
    virtuals = e_vir.shape[0]
    count = panel_of.shape[0]
    rows = panel // CHUNKS
    pos = lax.axis_index("virt").astype(jnp.int32).reshape(1)
    half = occ // 2

    def shift(x, d):
        return lax.ppermute(x, "virt", [(i, (i + d) % RING) for i in range(RING)])

    pieces = {}
    for part in range(2):
        mine = ints[part * half : (part + 1) * half]
        pieces[0, part] = mine
        up = down = mine
        for s in range(1, RING // 2 + 1):
            if s < RING // 2 or part == 0:
                up = shift(up, 1)
                pieces[s, part] = up
            if s < RING // 2 or part == 1:
                down = shift(down, -1)
                pieces[RING - s, part] = down
    held = [pieces[s, part] for s in range(RING) for part in range(2)]

    own = lax.all_to_all(amps, "virt", split_axis=0, concat_axis=0, tiled=True)
    own, *_ = lax.optimization_barrier([own] + [pieces[s, part] for s in (1, RING - 1) for part in range(2)])
    f32, bf16 = jnp.float32, jnp.bfloat16
    packed = jax.ShapeDtypeStruct((occ, count * rows // 2, 2 * panel), f32)
    direct, mirror = [], []
    for k in range(CHUNKS):
        amp_all = lax.all_gather(own[:, k * rows : (k + 1) * rows, :], "pair", axis=0)
        out = pl.pallas_call(
            functools.partial(product_kernel, (count, rows, occ, panel, width)),
            out_shape=packed,
            in_specs=[SMEM, SMEM, HBM] + [VMEM] * (2 * RING),
            out_specs=HBM,
            scratch_shapes=[
                pltpu.VMEM((count, RING, rows, width), f32),
                pltpu.VMEM((count * rows, RING * width), bf16),
                pltpu.VMEM((count * rows, RING * width), bf16),
                pltpu.VMEM((occ * panel, RING * width), bf16),
                pltpu.VMEM((occ * panel, RING * width), bf16),
                pltpu.VMEM((count * rows, occ * panel), f32),
                pltpu.VMEM(packed.shape, f32),
                pltpu.SemaphoreType.DMA,
                pltpu.SemaphoreType.DMA,
            ],
            compiler_params=pltpu.CompilerParams(vmem_limit_bytes=48 * 2**20),
            name=f"product_{k}",
        )(pos, panel_of, amp_all, *held)
        direct.append(out)
        mirror.append(lax.all_to_all(out, "virt", split_axis=0, concat_axis=0, tiled=True))

    e_b = lax.dynamic_slice(e_vir, (lax.axis_index("pair") * panel,), (panel,)).reshape(panel, 1)
    out = pl.pallas_call(
        functools.partial(finish_kernel, (rows, occ, panel, virtuals)),
        out_shape=jax.ShapeDtypeStruct((occ, panel, virtuals), f32),
        in_specs=[SMEM, SMEM, VMEM, VMEM] + [HBM] * (2 * CHUNKS),
        out_specs=HBM,
        scratch_shapes=[
            pltpu.VMEM((occ, CHUNKS) + packed.shape[1:], f32),
            pltpu.VMEM((occ, CHUNKS) + packed.shape[1:], f32),
            pltpu.VMEM((occ, panel, virtuals), f32),
            pltpu.SemaphoreType.DMA((occ, 2 * CHUNKS)),
            pltpu.SemaphoreType.DMA((occ,)),
        ],
        compiler_params=pltpu.CompilerParams(vmem_limit_bytes=48 * 2**20),
        name="finish",
    )(pos, e_occ, e_b, e_vir.reshape(1, virtuals), *direct, *mirror)
    return out[None]


def solution(mesh):
    in_specs = (P(None, "pair", "virt"), P(None, "pair", "virt"), P(), P(), P())
    out_specs = P("virt", None, "pair", None)
    return jax.shard_map(body, mesh=mesh, in_specs=in_specs, out_specs=out_specs, check_vma=False)
```

```python
import functools

import jax
import jax.numpy as jnp
from jax import lax
from jax.experimental import pallas as pl
from jax.experimental.pallas import tpu as pltpu
from jax.sharding import PartitionSpec as P

SIDE = 4
CORES = 2
NT = (((1,), (1,)), ((), ()))
SMEM = pl.BlockSpec(memory_space=pltpu.SMEM)
ANY = pl.BlockSpec(memory_space=pl.ANY)
VMEM = pl.BlockSpec(memory_space=pltpu.VMEM)
LIMIT = pltpu.CompilerParams(vmem_limit_bytes=48 * 2**20)
ROUTES = [
    [((1, 0), (1, 0)), ((-1, 0), (-1, 0)), ((0, 1), (0, 1)), ((0, -1), (0, -1))],
    [((1, 1), (1, 0)), ((-1, -1), (-1, 0)), ((-1, 1), (0, 1)), ((1, -1), (0, -1)), ((2, 0), (1, 0)), ((0, 2), (0, 1))],
    [((2, 1), (-1, 0)), ((1, 2), (0, -1)), ((2, -1), (1, 0)), ((-1, 2), (0, -1)), ((2, 2), (0, 1))],
]


def wrap(x, y):
    return x % SIDE, y % SIDE


def split(x):
    high = x.astype(jnp.bfloat16)
    return high, (x - high.astype(jnp.float32)).astype(jnp.bfloat16)


def product_kernel(dims, ints_hbm, *refs):
    depth, occ, panel, width, chips = dims
    amps_hbm = refs[:chips]
    out_hbm, ints, amps, i_hi, i_lo, a_hi, a_lo, out, int_sem, amp_sem, out_sem = refs[chips:]
    loads = [pltpu.make_async_copy(amps_hbm[g], amps.at[g], amp_sem.at[g]) for g in range(chips)]
    load = pltpu.make_async_copy(ints_hbm, ints, int_sem)
    load.start()
    for copy in loads:
        copy.start()
    load.wait()
    for s in range(depth):
        cols = slice(s * width, (s + 1) * width)
        i_hi[:, cols], i_lo[:, cols] = split(ints[s].reshape(occ * panel, width))
    for g in range(chips):
        loads[g].wait()
        for e in range(CORES):
            rows = slice((g * CORES + e) * panel, (g * CORES + e + 1) * panel)
            for s in range(depth):
                cols = slice(s * width, (s + 1) * width)
                a_hi[rows, cols], a_lo[rows, cols] = split(amps[g, e, s])
    dot = functools.partial(lax.dot_general, dimension_numbers=NT, preferred_element_type=jnp.float32)
    step = occ * panel // 2
    for m in range(2):
        at = slice(m * step, (m + 1) * step)
        sums = dot(i_hi[at], a_lo[...]) + dot(i_lo[at], a_hi[...]) + dot(i_hi[at], a_hi[...])
        out[m * occ // 2 : (m + 1) * occ // 2] = sums.reshape(occ // 2, panel, chips * CORES * panel)
    copy = pltpu.make_async_copy(out, out_hbm, out_sem)
    copy.start()
    copy.wait()


def finish_kernel(dims, slots, places, panel_of, e_occ, e_b, e_vir, *refs):
    occ, panel, virtuals, widths = dims
    chunks = len(widths)
    direct, mirror = refs[:chunks], refs[chunks : 2 * chunks]
    out_hbm, slot_of, dir_v, mir_v, out_v, in_sem, out_sem = refs[2 * chunks :]
    starts = [sum(widths[:k]) for k in range(chunks)]
    loads = []
    for j in range(occ):
        for k in range(chunks):
            cols = pl.ds(starts[k], widths[k])
            loads.append((j, pltpu.make_async_copy(direct[k].at[j], dir_v.at[j, :, cols], in_sem.at[j, k])))
            loads.append((j, pltpu.make_async_copy(mirror[k].at[j], mir_v.at[j, :, cols], in_sem.at[j, chunks + k])))
    for _, copy in loads:
        copy.start()
    v, x, y, core = places[0], places[1], places[2], places[3]
    for s, ((dx, dy), e) in enumerate(slots):
        chip = lax.rem(x + dx + SIDE, SIDE) * SIDE + lax.rem(y + dy + SIDE, SIDE)
        slot_of[panel_of[chip * CORES + lax.rem(core + e, CORES)]] = s
    lanes = 2 * panel
    lane = lax.broadcasted_iota(jnp.int32, (panel, lanes), 1)
    for j in range(occ):
        for at, copy in loads:
            if at == j:
                copy.wait()
        base = (e_occ[v] + e_occ[j]) - e_b[...]
        for t in range(virtuals // lanes):
            sides = []
            for h in range(2):
                s = slot_of[2 * t + h]
                cols = pl.ds(pl.multiple_of((s // 2) * lanes, lanes), lanes)
                diff = dir_v[j, :, cols] - mir_v[j, :, cols]
                sides.append(pltpu.roll(diff, lax.rem(s + h, 2) * panel, 1))
            cols = slice(t * lanes, (t + 1) * lanes)
            out_v[j, :, cols] = jnp.where(lane < panel, sides[0], sides[1]) / (base - e_vir[:, cols])
        pltpu.make_async_copy(out_v.at[j], out_hbm.at[j], out_sem.at[j]).start()
    for j in range(occ):
        pltpu.make_async_copy(out_v.at[j], out_hbm.at[j], out_sem.at[j]).wait()


def body(amps, ints, panel_of, e_occ, e_vir):
    occ, panel, width = amps.shape
    virtuals = e_vir.shape[0]
    depth = virtuals // width
    f32, bf16 = jnp.float32, jnp.bfloat16
    pair = lax.axis_index("pair").astype(jnp.int32)
    v = lax.axis_index("virt").astype(jnp.int32)
    places = jnp.stack([v, pair // (SIDE * CORES), (pair // CORES) % SIDE, pair % CORES])

    def move(data, dx, dy, dcore=0):
        perm = []
        for x in range(SIDE):
            for y in range(SIDE):
                for c in range(CORES):
                    to = wrap(x + dx, y + dy)
                    perm.append(((x * SIDE + y) * CORES + c, (to[0] * SIDE + to[1]) * CORES + (c + dcore) % CORES))
        return lax.ppermute(data, "pair", perm)

    int_all = lax.all_gather(ints, "virt", axis=0)
    own = lax.all_to_all(amps, "virt", split_axis=0, concat_axis=0, tiled=True)
    held = {(0, 0): jnp.stack([own, move(own, 0, 0, 1)])}
    slots, widths, direct, mirror = [], [], [], []
    for k, routes in enumerate(ROUTES):
        chips = [(0, 0)] if k == 0 else []
        for to, (dx, dy) in routes:
            before = wrap(to[0] - dx, to[1] - dy)
            held[wrap(*to)] = move(held[before], -dx, -dy)
            chips.append(wrap(*to))
        count = len(chips)
        slots += [(chip, e) for chip in chips for e in range(CORES)]
        widths.append(count * CORES * panel)
        shape = (occ, panel, widths[-1])
        out = pl.pallas_call(
            functools.partial(product_kernel, (depth, occ, panel, width, count)),
            out_shape=jax.ShapeDtypeStruct(shape, f32),
            in_specs=[ANY] * (1 + count),
            out_specs=ANY,
            scratch_shapes=[
                pltpu.VMEM((depth, occ, panel, width), f32),
                pltpu.VMEM((count, CORES, depth, panel, width), f32),
                pltpu.VMEM((occ * panel, depth * width), bf16),
                pltpu.VMEM((occ * panel, depth * width), bf16),
                pltpu.VMEM((widths[-1], depth * width), bf16),
                pltpu.VMEM((widths[-1], depth * width), bf16),
                pltpu.VMEM(shape, f32),
                pltpu.SemaphoreType.DMA,
                pltpu.SemaphoreType.DMA((count,)),
                pltpu.SemaphoreType.DMA,
            ],
            compiler_params=LIMIT,
            cost_estimate=pl.CostEstimate(flops=30_000_000_000, transcendentals=0, bytes_accessed=50_000_000),
            name=f"product_{k}",
        )(int_all, *[held[chip] for chip in chips])
        int_all, out, *mirror = lax.optimization_barrier((int_all, out, *mirror))
        direct.append(out)
        mirror.append(lax.all_to_all(out, "virt", split_axis=0, concat_axis=0, tiled=True))

    chunks = len(widths)
    e_b = lax.dynamic_slice(e_vir, (pair * panel,), (panel,)).reshape(panel, 1)
    out = pl.pallas_call(
        functools.partial(finish_kernel, (occ, panel, virtuals, tuple(widths)), slots),
        out_shape=jax.ShapeDtypeStruct((occ, panel, virtuals), f32),
        in_specs=[SMEM, SMEM, SMEM, VMEM, VMEM] + [ANY] * (2 * chunks),
        out_specs=ANY,
        scratch_shapes=[
            pltpu.SMEM((virtuals // panel,), jnp.int32),
            pltpu.VMEM((occ, panel, virtuals), f32),
            pltpu.VMEM((occ, panel, virtuals), f32),
            pltpu.VMEM((occ, panel, virtuals), f32),
            pltpu.SemaphoreType.DMA((occ, 2 * chunks)),
            pltpu.SemaphoreType.DMA((occ,)),
        ],
        compiler_params=LIMIT,
        name="finish",
    )(places, panel_of, e_occ, e_b, e_vir.reshape(1, virtuals), *direct, *mirror)
    return out[None]


def solution(mesh):
    in_specs = (P(None, "pair", "virt"), P(None, "pair", "virt"), P(), P(), P())
    out_specs = P("virt", None, "pair", None)
    return jax.shard_map(body, mesh=mesh, in_specs=in_specs, out_specs=out_specs, check_vma=False)
```

```python
import functools

import jax
import jax.numpy as jnp
from jax import lax
from jax.experimental import pallas as pl
from jax.experimental.pallas import tpu as pltpu
from jax.sharding import Mesh, PartitionSpec as P

SIDE = 4
CORES = 2
DEPTH = 8
EARLY = 10
NT = (((1,), (1,)), ((), ()))
SMEM = pl.BlockSpec(memory_space=pltpu.SMEM)
ANY = pl.BlockSpec(memory_space=pl.ANY)
VMEM = pl.BlockSpec(memory_space=pltpu.VMEM)
LIMIT = pltpu.CompilerParams(vmem_limit_bytes=60 * 2**20)
ROUTES = [
    [((1, 0), (1, 0)), ((-1, 0), (-1, 0)), ((0, 1), (0, 1)), ((0, -1), (0, -1)), ((1, 1), (1, 0))],
    [((-1, -1), (-1, 0)), ((-1, 1), (0, 1)), ((1, -1), (0, -1)), ((2, 0), (1, 0)), ((0, 2), (0, 1)), ((2, 1), (-1, 0)), ((1, 2), (0, -1)), ((2, -1), (1, 0)), ((-1, 2), (0, -1)), ((2, 2), (0, 1))],
]
SHIFTS = (4, 3, 5, 2, 6, 1, 7)


def wrap(x, y):
    return x % SIDE, y % SIDE


def split(x):
    high = x.astype(jnp.bfloat16)
    return high, (x - high.astype(jnp.float32)).astype(jnp.bfloat16)


def product_kernel(dims, whole, places, ints_hbm, *refs):
    occ, panel, width, chips = dims
    amps_hbm = refs[:chips]
    own_all, other_all = refs[chips : chips + 2]
    sends = refs[chips + 2 : -10]
    ints, amps, i_hi, i_lo, a_hi, a_lo, out, int_sem, amp_sem, out_sem = refs[-10:]
    loads = [pltpu.make_async_copy(amps_hbm[g], amps.at[g], amp_sem.at[g]) for g in range(chips)]
    int_loads = [pltpu.make_async_copy(ints_hbm.at[s], ints.at[s], int_sem.at[s]) for s in range(CORES * DEPTH)]
    for copy in loads + int_loads:
        copy.start()
    for g in range(chips):
        loads[g].wait()
        rows = slice(g * panel, (g + 1) * panel)
        for s in range(DEPTH):
            cols = slice(s * width, (s + 1) * width)
            a_hi[rows, cols], a_lo[rows, cols] = split(amps[g, s])
    height = occ * panel
    dot = functools.partial(lax.dot_general, dimension_numbers=NT, preferred_element_type=jnp.float32)
    core, v = places[3], places[0]
    for c in range(CORES):
        rows = slice(c * height, (c + 1) * height)
        for s in range(DEPTH):
            int_loads[c * DEPTH + s].wait()
            cols = slice(s * width, (s + 1) * width)
            i_hi[rows, cols], i_lo[rows, cols] = split(ints[c * DEPTH + s].reshape(height, width))
        sums = dot(i_hi[rows], a_lo[...]) + dot(i_lo[rows], a_hi[...]) + dot(i_hi[rows], a_hi[...])
        out[c * occ : (c + 1) * occ] = sums.reshape(occ, panel, chips * panel)
    copies = [(out, sends[0])] if whole else []
    for d in range(occ):
        j = lax.rem(v + d, occ)
        own, other = out.at[core * occ + j], out.at[(1 - core) * occ + j]
        copies.append((own, own_all.at[d]))
        copies.append((other, other_all.at[d]))
        if d > 0 and not whole:
            copies.append((own, sends[2 * (d - 1)]))
            copies.append((other, sends[2 * (d - 1) + 1]))
    copies = [pltpu.make_async_copy(a, b, out_sem.at[n]) for n, (a, b) in enumerate(copies)]
    for copy in copies:
        copy.start()
    for copy in copies:
        copy.wait()


def finish_kernel(dims, slots, places, panel_of, e_occ, e_b, e_vir, *refs):
    occ, panel, virtuals, widths = dims
    chunks = len(widths)
    first, second = refs[: CORES + 1], refs[CORES + 1 : -7]
    out_hbm, slot_of, dir_v, mir_v, out_v, in_sem, out_sem = refs[-7:]
    v, x, y, core = places[0], places[1], places[2], places[3]
    loads = []
    for d in range(occ):
        mine = []
        for k in range(chunks):
            part = second if k else first
            for e in range(CORES):
                cols = pl.ds(e * virtuals // 2 + sum(widths[:k]), widths[k])
                mine.append((part[e].at[d], dir_v.at[d, :, cols]))
                if d > 0:
                    if k:
                        source = part[CORES + 2 * (d - 1) + e]
                    else:
                        source = part[CORES].at[lax.rem(core + e, CORES) * occ + lax.rem(v + d, occ)]
                    mine.append((source, mir_v.at[d, :, cols]))
        loads.append([pltpu.make_async_copy(a, b, in_sem.at[d, n]) for n, (a, b) in enumerate(mine)])
        for copy in loads[d]:
            copy.start()
    for s, ((dx, dy), e) in enumerate(slots):
        chip = lax.rem(x + dx, SIDE) * SIDE + lax.rem(y + dy, SIDE)
        slot_of[panel_of[chip * CORES + lax.rem(core + e, CORES)]] = s
    lanes = 2 * panel
    lane = lax.broadcasted_iota(jnp.int32, (panel, lanes), 1)
    for d in range(occ):
        for copy in loads[d]:
            copy.wait()
        j = lax.rem(v + d, occ)
        other = mir_v if d > 0 else dir_v
        base = (e_occ[v] + e_occ[j]) - e_b[...]
        for t in range(virtuals // lanes):
            sides = []
            for h in range(2):
                s = slot_of[2 * t + h]
                cols = pl.ds(pl.multiple_of((s // 2) * lanes, lanes), lanes)
                diff = dir_v[d, :, cols] - other[d, :, cols]
                sides.append(pltpu.roll(diff, lax.rem(s + h, 2) * panel, 1))
            cols = slice(t * lanes, (t + 1) * lanes)
            out_v[d, :, cols] = jnp.where(lane < panel, sides[0], sides[1]) / (base - e_vir[:, cols])
        pltpu.make_async_copy(out_v.at[d], out_hbm.at[j], out_sem.at[d]).start()
    for d in range(occ):
        j = lax.rem(v + d, occ)
        pltpu.make_async_copy(out_v.at[d], out_hbm.at[j], out_sem.at[d]).wait()


def body(amps, ints, panel_of, e_occ, e_vir):
    occ, panel, width = amps.shape
    virtuals = e_vir.shape[0]
    f32, bf16 = jnp.float32, jnp.bfloat16
    index = [lax.axis_index(name).astype(jnp.int32) for name in ("virt", "x", "y", "core")]
    places = jnp.stack(index)

    def move(data, dx, dy):
        name, step = ("x", dx) if dx else ("y", dy)
        return lax.ppermute(data, name, [(n, (n - step) % SIDE) for n in range(SIDE)])

    def cross(data, dcore, d):
        perm = [(c * DEPTH + z, (c + dcore) % CORES * DEPTH + (z + d) % DEPTH) for c in range(CORES) for z in range(DEPTH)]
        return lax.ppermute(data, ("core", "virt"), perm)

    int_all = lax.all_gather(ints, ("core", "virt"), axis=0)
    held = {(0, 0): lax.all_to_all(amps, "virt", split_axis=0, concat_axis=0, tiled=True)}
    chips_of, widths, arrays = [], [], []
    for k, routes in enumerate(ROUTES):
        chips = [(0, 0)] if k == 0 else []
        for to, (dx, dy) in routes:
            held[wrap(*to)] = move(held[wrap(to[0] - dx, to[1] - dy)], dx, dy)
            chips.append(wrap(*to))
        count = len(chips)
        chips_of += chips
        widths.append(count * panel)
        one = jax.ShapeDtypeStruct((panel, widths[-1]), f32)
        every = jax.ShapeDtypeStruct((occ,) + one.shape, f32)
        both = jax.ShapeDtypeStruct((CORES * occ,) + one.shape, f32)
        height = CORES * occ * panel
        shapes = [every] * CORES + ([one] * (2 * (occ - 1)) if k else [both])
        own_all, other_all, *sends = pl.pallas_call(
            functools.partial(product_kernel, (occ, panel, width, count), k == 0),
            out_shape=shapes,
            in_specs=[SMEM] + [ANY] * (1 + count),
            out_specs=[ANY] * len(shapes),
            scratch_shapes=[
                pltpu.VMEM((CORES * DEPTH, occ, panel, width), f32),
                pltpu.VMEM((count, DEPTH, panel, width), f32),
                pltpu.VMEM((height, DEPTH * width), bf16),
                pltpu.VMEM((height, DEPTH * width), bf16),
                pltpu.VMEM((widths[-1], DEPTH * width), bf16),
                pltpu.VMEM((widths[-1], DEPTH * width), bf16),
                pltpu.VMEM(both.shape, f32),
                pltpu.SemaphoreType.DMA((CORES * DEPTH,)),
                pltpu.SemaphoreType.DMA((count,)),
                pltpu.SemaphoreType.DMA((4 * occ,)),
            ],
            compiler_params=LIMIT,
            cost_estimate=pl.CostEstimate(flops=20_000_000_000, transcendentals=0, bytes_accessed=30_000_000),
            name=f"product_{k}",
        )(places, int_all, *[held[chip] for chip in chips])
        if k == 0:
            early = lax.all_to_all(sends[0], ("core", "virt"), split_axis=0, concat_axis=0, tiled=True)
            int_all, other_all = lax.optimization_barrier((int_all, other_all))
            early_other = other_all
            arrays += [own_all]
            continue
        mirror = {}
        order = [(d, e) for d in SHIFTS for e in range(CORES)]
        order.remove((SHIFTS[0], 1))
        order.append((SHIFTS[0], 1))
        late = [sends[2 * (d - 1) + e] for d, e in order[EARLY:]]
        early, other_all, *late = lax.optimization_barrier((early, other_all, *late))
        for n, (d, e) in enumerate(order):
            mirror[occ - d, e] = cross(late[n - EARLY] if n >= EARLY else sends[2 * (d - 1) + e], e, d)
        arrays += [cross(early_other, 1, 0), early, own_all, cross(other_all, 1, 0)]
        arrays += [mirror[d, e] for d in range(1, occ) for e in range(CORES)]

    slots = [(chip, e) for e in range(CORES) for chip in chips_of]
    chunks = len(widths)
    pair = (index[1] * SIDE + index[2]) * CORES + index[3]
    e_b = lax.dynamic_slice(e_vir, (pair * panel,), (panel,)).reshape(panel, 1)
    out = pl.pallas_call(
        functools.partial(finish_kernel, (occ, panel, virtuals, tuple(widths)), slots),
        out_shape=jax.ShapeDtypeStruct((occ, panel, virtuals), f32),
        in_specs=[SMEM, SMEM, SMEM, VMEM, VMEM] + [ANY] * len(arrays),
        out_specs=ANY,
        scratch_shapes=[
            pltpu.SMEM((virtuals // panel,), jnp.int32),
            pltpu.VMEM((occ, panel, virtuals), f32),
            pltpu.VMEM((occ, panel, virtuals), f32),
            pltpu.VMEM((occ, panel, virtuals), f32),
            pltpu.SemaphoreType.DMA((occ, 2 * CORES * chunks)),
            pltpu.SemaphoreType.DMA((occ,)),
        ],
        compiler_params=LIMIT,
        name="finish",
    )(places, panel_of, e_occ, e_b, e_vir.reshape(1, virtuals), *arrays)
    return out[None]


def solution(mesh):
    fine = Mesh(mesh.devices.reshape(SIDE, SIDE, CORES, DEPTH), ("x", "y", "core", "virt"))
    rows = ("x", "y", "core")
    in_specs = (P(None, rows, "virt"), P(None, rows, "virt"), P(), P(), P())
    out_specs = P("virt", None, rows, None)
    return jax.shard_map(body, mesh=fine, in_specs=in_specs, out_specs=out_specs, check_vma=False)
```

```python
import functools

import jax
import jax.numpy as jnp
from jax import lax
from jax.experimental import pallas as pl
from jax.experimental.pallas import tpu as pltpu
from jax.sharding import Mesh, PartitionSpec as P

SIDE = 4
CORES = 2
DEPTH = 8
HALVES = 2
BLOCK = 256
NT = (((1,), (1,)), ((), ()))
SMEM = pl.BlockSpec(memory_space=pltpu.SMEM)
ANY = pl.BlockSpec(memory_space=pl.ANY)
VMEM = pl.BlockSpec(memory_space=pltpu.VMEM)
LIMIT = pltpu.CompilerParams(vmem_limit_bytes=60 * 2**20)
COSTS = [pl.CostEstimate(flops=f * 10**9, transcendentals=0, bytes_accessed=20_000_000) for f in (40, 2, 40)]
ROUTES = [
    [((1, 0), (1, 0)), ((-1, 0), (-1, 0)), ((0, 1), (0, 1)), ((0, -1), (0, -1)), ((1, 1), (1, 0)), ((-1, -1), (-1, 0)), ((-1, 1), (0, 1))],
    [((1, -1), (0, -1)), ((2, 0), (1, 0)), ((0, 2), (0, 1)), ((2, 1), (-1, 0)), ((1, 2), (0, -1)), ((2, -1), (1, 0)), ((-1, 2), (0, -1)), ((2, 2), (0, 1))],
]
PIECES = [(0, (0,)), (0, (1,)), (1, (0, 1))]


def wrap(x, y):
    return x % SIDE, y % SIDE


def split(x):
    high = x.astype(jnp.bfloat16)
    return high, (x - high.astype(jnp.float32)).astype(jnp.bfloat16)


def product_kernel(dims, places, *refs):
    occ, part, panel, width, parts, chips = dims
    ints_hbm, amps_hbm = refs[:parts], refs[parts : parts + chips]
    own_all, other_all, whole = refs[parts + chips : parts + chips + 3]
    ints, amps, i_hi, i_lo, a_hi, a_lo, out, int_sem, amp_sem, out_sem = refs[parts + chips + 3 :]
    loads = [pltpu.make_async_copy(amps_hbm[g], amps.at[g], amp_sem.at[g]) for g in range(chips)]
    int_loads = [
        pltpu.make_async_copy(ints_hbm[h].at[s], ints.at[h, s], int_sem.at[h, s])
        for h in range(parts)
        for s in range(CORES * DEPTH)
    ]
    for copy in loads + int_loads:
        copy.start()
    for g in range(chips):
        loads[g].wait()
        rows = slice(g * panel, (g + 1) * panel)
        for s in range(DEPTH):
            cols = slice(s * width, (s + 1) * width)
            a_hi[rows, cols], a_lo[rows, cols] = split(amps[g, s])
    height = occ * part
    dot = functools.partial(lax.dot_general, dimension_numbers=NT, preferred_element_type=jnp.float32)
    for h in range(parts):
        for c in range(CORES):
            for s in range(DEPTH):
                int_loads[(h * CORES + c) * DEPTH + s].wait()
                cols = slice(s * width, (s + 1) * width)
                i_hi[:, cols], i_lo[:, cols] = split(ints[h, c * DEPTH + s].reshape(height, width))
            for m in range(0, height, BLOCK):
                at = slice(m, m + BLOCK)
                sums = dot(i_hi[at], a_lo[...]) + dot(i_lo[at], a_hi[...]) + dot(i_hi[at], a_hi[...])
                at = slice(c * occ + m // part, c * occ + (m + BLOCK) // part)
                out[at, h * part : (h + 1) * part, :] = sums.reshape(BLOCK // part, part, chips * panel)
    core = places[3]
    copies = [
        pltpu.make_async_copy(out, whole, out_sem.at[0]),
        pltpu.make_async_copy(out.at[pl.ds(core * occ, occ)], own_all, out_sem.at[1]),
        pltpu.make_async_copy(out.at[pl.ds((1 - core) * occ, occ)], other_all, out_sem.at[2]),
    ]
    for copy in copies:
        copy.start()
    for copy in copies:
        copy.wait()


def finish_kernel(dims, pieces, slots, places, panel_of, e_occ, e_b, e_vir, *refs):
    occ, panel, virtuals = dims
    out_hbm, slot_of, dir_v, mir_v, out_v, in_sem, out_sem = refs[3 * len(pieces) :]
    v, x, y, core = places[0], places[1], places[2], places[3]
    loads = []
    for j in range(occ):
        mine = []
        for n, (first, size, rows, height) in enumerate(pieces):
            own, other, mirror = refs[3 * n : 3 * n + 3]
            for e in range(CORES):
                at = (j, pl.ds(rows, height), pl.ds(e * virtuals // 2 + first, size))
                mine.append(((other if e else own).at[j], dir_v.at[at]))
                mine.append((mirror.at[lax.rem(core + e, CORES) * occ + j], mir_v.at[at]))
        loads.append([pltpu.make_async_copy(a, b, in_sem.at[j, n]) for n, (a, b) in enumerate(mine)])
        for copy in loads[j]:
            copy.start()
    for s, ((dx, dy), e) in enumerate(slots):
        chip = lax.rem(x + dx, SIDE) * SIDE + lax.rem(y + dy, SIDE)
        slot_of[panel_of[chip * CORES + lax.rem(core + e, CORES)]] = s
    lanes = 2 * panel
    lane = lax.broadcasted_iota(jnp.int32, (panel, lanes), 1)
    for j in range(occ):
        for copy in loads[j]:
            copy.wait()
        base = (e_occ[v] + e_occ[j]) - e_b[...]
        for t in range(virtuals // lanes):
            sides = []
            for h in range(2):
                s = slot_of[2 * t + h]
                cols = pl.ds(pl.multiple_of((s // 2) * lanes, lanes), lanes)
                diff = dir_v[j, :, cols] - mir_v[j, :, cols]
                sides.append(pltpu.roll(diff, lax.rem(s + h, 2) * panel, 1))
            cols = slice(t * lanes, (t + 1) * lanes)
            out_v[j, :, cols] = jnp.where(lane < panel, sides[0], sides[1]) / (base - e_vir[:, cols])
        pltpu.make_async_copy(out_v.at[j], out_hbm.at[j], out_sem.at[j]).start()
    for j in range(occ):
        pltpu.make_async_copy(out_v.at[j], out_hbm.at[j], out_sem.at[j]).wait()


def body(amps, ints, panel_of, e_occ, e_vir):
    occ, panel, width = amps.shape
    virtuals = e_vir.shape[0]
    f32, bf16 = jnp.float32, jnp.bfloat16
    index = [lax.axis_index(name).astype(jnp.int32) for name in ("virt", "x", "y", "core")]
    places = jnp.stack(index)
    part = panel // HALVES

    def move(data, dx, dy):
        name, step = ("x", dx) if dx else ("y", dy)
        return lax.ppermute(data, name, [(n, (n - step) % SIDE) for n in range(SIDE)])

    int_all = [lax.all_gather(ints[:, h * part : (h + 1) * part], ("core", "virt"), axis=0) for h in range(HALVES)]
    held = {(0, 0): lax.all_to_all(amps, "virt", split_axis=0, concat_axis=0, tiled=True)}
    sets, starts = [], []
    for k, routes in enumerate(ROUTES):
        chips = [(0, 0)] if k == 0 else []
        for to, (dx, dy) in routes:
            held[wrap(*to)] = move(held[wrap(to[0] - dx, to[1] - dy)], dx, dy)
            chips.append(wrap(*to))
        starts.append(sum(map(len, sets)) * panel)
        sets.append(chips)

    arrays, places_of, mirror = [], [], []
    for n, (k, halves) in enumerate(PIECES):
        chips, parts = sets[k], len(halves)
        size, tall = len(chips) * panel, parts * part
        every = jax.ShapeDtypeStruct((occ, tall, size), f32)
        both = jax.ShapeDtypeStruct((CORES * occ, tall, size), f32)
        own_all, other_all, whole = pl.pallas_call(
            functools.partial(product_kernel, (occ, part, panel, width, parts, len(chips))),
            out_shape=[every, every, both],
            in_specs=[SMEM] + [ANY] * (parts + len(chips)),
            out_specs=[ANY] * 3,
            scratch_shapes=[
                pltpu.VMEM((parts, CORES * DEPTH, occ, part, width), f32),
                pltpu.VMEM((len(chips), DEPTH, panel, width), f32),
                pltpu.VMEM((occ * part, DEPTH * width), bf16),
                pltpu.VMEM((occ * part, DEPTH * width), bf16),
                pltpu.VMEM((size, DEPTH * width), bf16),
                pltpu.VMEM((size, DEPTH * width), bf16),
                pltpu.VMEM(both.shape, f32),
                pltpu.SemaphoreType.DMA((parts, CORES * DEPTH)),
                pltpu.SemaphoreType.DMA((len(chips),)),
                pltpu.SemaphoreType.DMA((3,)),
            ],
            compiler_params=LIMIT,
            cost_estimate=COSTS[n],
            name=f"product_{n}",
        )(places, *[int_all[h] for h in halves], *[held[chip] for chip in chips])
        if mirror:
            whole, mirror[-1] = lax.optimization_barrier((whole, mirror[-1]))
        mirror.append(lax.all_to_all(whole, ("core", "virt"), split_axis=0, concat_axis=0, tiled=True))
        arrays.append([own_all, lax.ppermute(other_all, "core", [(0, 1), (1, 0)])])
        places_of.append((starts[k], size, halves[0] * part, tall))
        if n + 1 < len(PIECES):
            after = [own_all] + mirror[:-1]
            tied = lax.optimization_barrier(int_all + after)
            int_all = list(tied[:HALVES])
    for pair_of, back in zip(arrays, mirror):
        pair_of.append(back)

    slots = [(chip, e) for e in range(CORES) for chips in sets for chip in chips]
    pair = (index[1] * SIDE + index[2]) * CORES + index[3]
    e_b = lax.dynamic_slice(e_vir, (pair * panel,), (panel,)).reshape(panel, 1)
    out = pl.pallas_call(
        functools.partial(finish_kernel, (occ, panel, virtuals), places_of, slots),
        out_shape=jax.ShapeDtypeStruct((occ, panel, virtuals), f32),
        in_specs=[SMEM, SMEM, SMEM, VMEM, VMEM] + [ANY] * (3 * len(PIECES)),
        out_specs=ANY,
        scratch_shapes=[
            pltpu.SMEM((virtuals // panel,), jnp.int32),
            pltpu.VMEM((occ, panel, virtuals), f32),
            pltpu.VMEM((occ, panel, virtuals), f32),
            pltpu.VMEM((occ, panel, virtuals), f32),
            pltpu.SemaphoreType.DMA((occ, 2 * CORES * len(PIECES))),
            pltpu.SemaphoreType.DMA((occ,)),
        ],
        compiler_params=LIMIT,
        name="finish",
    )(places, panel_of, e_occ, e_b, e_vir.reshape(1, virtuals), *[a for group in arrays for a in group])
    return out[None]


def solution(mesh):
    fine = Mesh(mesh.devices.reshape(SIDE, SIDE, CORES, DEPTH), ("x", "y", "core", "virt"))
    rows = ("x", "y", "core")
    in_specs = (P(None, rows, "virt"), P(None, rows, "virt"), P(), P(), P())
    out_specs = P("virt", None, rows, None)
    return jax.shard_map(body, mesh=fine, in_specs=in_specs, out_specs=out_specs, check_vma=False)
```

```python
import functools

import jax
import jax.numpy as jnp
from jax import lax
from jax.experimental import pallas as pl
from jax.experimental.pallas import tpu as pltpu
from jax.sharding import Mesh, PartitionSpec as P

SIDE = 4
CORES = 2
DEPTH = 8
HALVES = 1
BLOCK = 256
NT = (((1,), (1,)), ((), ()))
SMEM = pl.BlockSpec(memory_space=pltpu.SMEM)
ANY = pl.BlockSpec(memory_space=pl.ANY)
VMEM = pl.BlockSpec(memory_space=pltpu.VMEM)
HBM = pl.BlockSpec(memory_space=pltpu.HBM)
LIMIT = pltpu.CompilerParams(vmem_limit_bytes=60 * 2**20)
COSTS = [pl.CostEstimate(flops=f * 10**9, transcendentals=0, bytes_accessed=f * 10**6) for f in (20, 40)]
FIRST = [
    ((1, 0), (1, 0)),
    ((-1, 0), (-1, 0)),
    ((0, 1), (0, 1)),
    ((0, -1), (0, -1)),
    ((1, 1), (1, 0)),
    ((-1, -1), (-1, 0)),
    ((-1, 1), (0, 1)),
    ((1, -1), (0, -1)),
    ((2, 0), (1, 0)),
    ((0, 2), (0, 1)),
    ((2, 1), (-1, 0)),
    ((1, 2), (0, -1)),
]
LAST = [((2, -1), (1, 0)), ((-1, 2), (0, -1)), ((2, 2), (0, 1))]
SETS = [
    [(0, 0), (1, 0), (-1, 0), (0, 1)],
    [(0, -1), (1, 1), (-1, -1), (-1, 1), (1, -1), (2, 0), (0, 2), (2, 1), (1, 2), (2, -1), (-1, 2), (2, 2)],
]
SOON = [(1, 1), (-1, -1), (-1, 1), (1, -1)]
PIECES = [(0, (0,)), (1, (0,))]


def wrap(x, y):
    return x % SIDE, y % SIDE


def split(x):
    high = x.astype(jnp.bfloat16)
    return high, (x - high.astype(jnp.float32)).astype(jnp.bfloat16)


def product_kernel(dims, places, *refs):
    occ, part, panel, width, parts, chips = dims
    ints_hbm, amps_hbm = refs[:parts], refs[parts : parts + chips]
    own_all, other_all, whole = refs[parts + chips : parts + chips + 3]
    ints, amps, i_hi, i_lo, a_hi, a_lo, out, int_sem, amp_sem, out_sem = refs[parts + chips + 3 :]
    loads = [pltpu.make_async_copy(amps_hbm[g], amps.at[g], amp_sem.at[g]) for g in range(chips)]
    int_loads = [
        pltpu.make_async_copy(ints_hbm[h].at[s], ints.at[h, s], int_sem.at[h, s])
        for h in range(parts)
        for s in range(CORES * DEPTH)
    ]
    for copy in loads + int_loads:
        copy.start()
    for g in range(chips):
        loads[g].wait()
        rows = slice(g * panel, (g + 1) * panel)
        for s in range(DEPTH):
            cols = slice(s * width, (s + 1) * width)
            a_hi[rows, cols], a_lo[rows, cols] = split(amps[g, s])
    height = occ * part
    dot = functools.partial(lax.dot_general, dimension_numbers=NT, preferred_element_type=jnp.float32)
    for h in range(parts):
        for c in range(CORES):
            for s in range(DEPTH):
                int_loads[(h * CORES + c) * DEPTH + s].wait()
                cols = slice(s * width, (s + 1) * width)
                i_hi[:, cols], i_lo[:, cols] = split(ints[h, c * DEPTH + s].reshape(height, width))
            for m in range(0, height, BLOCK):
                at = slice(m, m + BLOCK)
                sums = dot(i_hi[at], a_lo[...]) + dot(i_lo[at], a_hi[...]) + dot(i_hi[at], a_hi[...])
                at = slice(c * occ + m // part, c * occ + (m + BLOCK) // part)
                out[at, h * part : (h + 1) * part, :] = sums.reshape(BLOCK // part, part, chips * panel)
    core = places[3]
    copies = [
        pltpu.make_async_copy(out, whole, out_sem.at[0]),
        pltpu.make_async_copy(out.at[pl.ds(core * occ, occ)], own_all, out_sem.at[1]),
        pltpu.make_async_copy(out.at[pl.ds((1 - core) * occ, occ)], other_all, out_sem.at[2]),
    ]
    for copy in copies:
        copy.start()
    for copy in copies:
        copy.wait()


def finish_kernel(dims, pieces, slots, places, panel_of, e_occ, e_b, e_vir, *refs):
    occ, panel, virtuals = dims
    out_hbm, slot_of, dir_v, mir_v, out_v, in_sem, out_sem = refs[3 * len(pieces) :]
    v, x, y, core = places[0], places[1], places[2], places[3]
    loads = []
    for j in range(occ):
        mine = []
        for n, (first, size, rows, height) in enumerate(pieces):
            own, other, mirror = refs[3 * n : 3 * n + 3]
            for e in range(CORES):
                at = (j, pl.ds(rows, height), pl.ds(e * virtuals // 2 + first, size))
                mine.append(((other if e else own).at[j], dir_v.at[at]))
                mine.append((mirror.at[lax.rem(core + e, CORES) * occ + j], mir_v.at[at]))
        loads.append([pltpu.make_async_copy(a, b, in_sem.at[j, n]) for n, (a, b) in enumerate(mine)])
        for copy in loads[j]:
            copy.start()
    for s, ((dx, dy), e) in enumerate(slots):
        chip = lax.rem(x + dx, SIDE) * SIDE + lax.rem(y + dy, SIDE)
        slot_of[panel_of[chip * CORES + lax.rem(core + e, CORES)]] = s
    lanes = 2 * panel
    lane = lax.broadcasted_iota(jnp.int32, (panel, lanes), 1)
    for j in range(occ):
        for copy in loads[j]:
            copy.wait()
        base = (e_occ[v] + e_occ[j]) - e_b[...]
        for t in range(virtuals // lanes):
            sides = []
            for h in range(2):
                s = slot_of[2 * t + h]
                cols = pl.ds(pl.multiple_of((s // 2) * lanes, lanes), lanes)
                diff = dir_v[j, :, cols] - mir_v[j, :, cols]
                sides.append(pltpu.roll(diff, lax.rem(s + h, 2) * panel, 1))
            cols = slice(t * lanes, (t + 1) * lanes)
            out_v[j, :, cols] = jnp.where(lane < panel, sides[0], sides[1]) / (base - e_vir[:, cols])
        pltpu.make_async_copy(out_v.at[j], out_hbm.at[j], out_sem.at[j]).start()
    for j in range(occ):
        pltpu.make_async_copy(out_v.at[j], out_hbm.at[j], out_sem.at[j]).wait()


def body(amps, ints, panel_of, e_occ, e_vir):
    occ, panel, width = amps.shape
    virtuals = e_vir.shape[0]
    f32, bf16 = jnp.float32, jnp.bfloat16
    index = [lax.axis_index(name).astype(jnp.int32) for name in ("virt", "x", "y", "core")]
    places = jnp.stack(index)
    part = panel // HALVES

    def move(data, dx, dy):
        name, step = ("x", dx) if dx else ("y", dy)
        return lax.ppermute(data, name, [(n, (n - step) % SIDE) for n in range(SIDE)])

    int_all = [lax.all_gather(ints[:, h * part : (h + 1) * part], ("core", "virt"), axis=0) for h in range(HALVES)]
    held = {(0, 0): lax.all_to_all(amps, "virt", split_axis=0, concat_axis=0, tiled=True)}
    sets = [[wrap(*chip) for chip in chips] for chips in SETS]
    starts = [sum(map(len, sets[:k])) * panel for k in range(len(sets))]

    def bring(routes, after=()):
        for to, (dx, dy) in routes:
            data = held[wrap(to[0] - dx, to[1] - dy)]
            if after:
                data = lax.optimization_barrier([data, *after])[0]
            held[wrap(*to)] = move(data, dx, dy)

    bring(FIRST)
    soon = [wrap(*chip) for chip in SOON]
    int_all[0], *ready = lax.optimization_barrier([int_all[0]] + [held[chip] for chip in soon])
    held.update(zip(soon, ready))

    arrays, places_of, mirror = [], [], []
    for n, (k, halves) in enumerate(PIECES):
        chips, parts = sets[k], len(halves)
        size, tall = len(chips) * panel, parts * part
        every = jax.ShapeDtypeStruct((occ, tall, size), f32)
        both = jax.ShapeDtypeStruct((CORES * occ, tall, size), f32)
        own_all, other_all, whole = pl.pallas_call(
            functools.partial(product_kernel, (occ, part, panel, width, parts, len(chips))),
            out_shape=[every, every, both],
            in_specs=[SMEM] + [ANY] * (parts + len(chips)),
            out_specs=[ANY] * 3,
            scratch_shapes=[
                pltpu.VMEM((parts, CORES * DEPTH, occ, part, width), f32),
                pltpu.VMEM((len(chips), DEPTH, panel, width), f32),
                pltpu.VMEM((occ * part, DEPTH * width), bf16),
                pltpu.VMEM((occ * part, DEPTH * width), bf16),
                pltpu.VMEM((size, DEPTH * width), bf16),
                pltpu.VMEM((size, DEPTH * width), bf16),
                pltpu.VMEM(both.shape, f32),
                pltpu.SemaphoreType.DMA((parts, CORES * DEPTH)),
                pltpu.SemaphoreType.DMA((len(chips),)),
                pltpu.SemaphoreType.DMA((3,)),
            ],
            compiler_params=LIMIT,
            cost_estimate=COSTS[n],
            name=f"product_{n}",
        )(places, *[int_all[h] for h in halves], *[held[chip] for chip in chips])
        if mirror:
            whole, mirror[-1] = lax.optimization_barrier((whole, mirror[-1]))
        mirror.append(lax.all_to_all(whole, ("core", "virt"), split_axis=0, concat_axis=0, tiled=True))
        arrays.append([own_all, lax.ppermute(other_all, "core", [(0, 1), (1, 0)])])
        places_of.append((starts[k], size, halves[0] * part, tall))
        if n + 1 < len(PIECES):
            int_all = list(lax.optimization_barrier(int_all + [own_all])[:HALVES])
            bring(LAST, [own_all])
    for pair_of, back in zip(arrays, mirror):
        pair_of.append(back)

    slots = [(chip, e) for e in range(CORES) for chips in sets for chip in chips]
    pair = (index[1] * SIDE + index[2]) * CORES + index[3]
    e_b = lax.dynamic_slice(e_vir, (pair * panel,), (panel,)).reshape(panel, 1)
    out = pl.pallas_call(
        functools.partial(finish_kernel, (occ, panel, virtuals), places_of, slots),
        out_shape=jax.ShapeDtypeStruct((occ, panel, virtuals), f32),
        in_specs=[SMEM, SMEM, SMEM, VMEM, VMEM] + [HBM] * (3 * len(PIECES) - 1) + [VMEM],
        out_specs=ANY,
        scratch_shapes=[
            pltpu.SMEM((virtuals // panel,), jnp.int32),
            pltpu.VMEM((occ, panel, virtuals), f32),
            pltpu.VMEM((occ, panel, virtuals), f32),
            pltpu.VMEM((occ, panel, virtuals), f32),
            pltpu.SemaphoreType.DMA((occ, 2 * CORES * len(PIECES))),
            pltpu.SemaphoreType.DMA((occ,)),
        ],
        compiler_params=pltpu.CompilerParams(vmem_limit_bytes=60 * 2**20),
        name="finish",
    )(places, panel_of, e_occ, e_b, e_vir.reshape(1, virtuals), *[a for group in arrays for a in group])
    return out[None]


def solution(mesh):
    fine = Mesh(mesh.devices.reshape(SIDE, SIDE, CORES, DEPTH), ("x", "y", "core", "virt"))
    rows = ("x", "y", "core")
    in_specs = (P(None, rows, "virt"), P(None, rows, "virt"), P(), P(), P())
    out_specs = P("virt", None, rows, None)
    return jax.shard_map(body, mesh=fine, in_specs=in_specs, out_specs=out_specs, check_vma=False)
```

```python
import functools

import jax
import jax.numpy as jnp
from jax import lax
from jax.experimental import pallas as pl
from jax.experimental.pallas import tpu as pltpu
from jax.sharding import Mesh, PartitionSpec as P

SIDE = 4
CORES = 2
DEPTH = 8
HALVES = 1
BLOCK = 256
NT = (((1,), (1,)), ((), ()))
SMEM = pl.BlockSpec(memory_space=pltpu.SMEM)
ANY = pl.BlockSpec(memory_space=pl.ANY)
VMEM = pl.BlockSpec(memory_space=pltpu.VMEM)
HBM = pl.BlockSpec(memory_space=pltpu.HBM)
LIMIT = pltpu.CompilerParams(vmem_limit_bytes=60 * 2**20)
COSTS = [pl.CostEstimate(flops=f * 10**9, transcendentals=0, bytes_accessed=f * 10**6) for f in (60, 8)]
FIRST = [
    ((1, 0), (1, 0)),
    ((-1, 0), (-1, 0)),
    ((0, 1), (0, 1)),
    ((0, -1), (0, -1)),
    ((1, 1), (1, 0)),
    ((-1, -1), (-1, 0)),
    ((-1, 1), (0, 1)),
    ((1, -1), (0, -1)),
    ((2, 0), (1, 0)),
    ((0, 2), (0, 1)),
    ((2, 1), (-1, 0)),
    ((1, 2), (0, -1)),
]
LAST = [((2, -1), (1, 0)), ((-1, 2), (0, -1)), ((2, 2), (0, 1))]
SETS = [
    [(0, 0), (1, 0), (-1, 0), (0, 1), (0, -1), (1, 1), (-1, -1), (-1, 1)],
    [(1, -1), (2, 0), (0, 2), (2, 1), (1, 2), (2, -1), (-1, 2), (2, 2)],
]
SOON = [(1, 1), (-1, -1), (-1, 1), (1, -1)]
PIECES = [(0, (0,)), (1, (0,))]


def wrap(x, y):
    return x % SIDE, y % SIDE


def split(x):
    high = x.astype(jnp.bfloat16)
    return high, (x - high.astype(jnp.float32)).astype(jnp.bfloat16)


def product_kernel(dims, places, *refs):
    occ, part, panel, width, parts, chips = dims
    ints_hbm, amps_hbm = refs[:parts], refs[parts : parts + chips]
    own_all, other_all, whole = refs[parts + chips : parts + chips + 3]
    ints, amps, i_hi, i_lo, a_hi, a_lo, out, int_sem, amp_sem, out_sem = refs[parts + chips + 3 :]
    loads = [pltpu.make_async_copy(amps_hbm[g], amps.at[g], amp_sem.at[g]) for g in range(chips)]
    int_loads = [
        pltpu.make_async_copy(ints_hbm[h].at[s], ints.at[h, s], int_sem.at[h, s])
        for h in range(parts)
        for s in range(CORES * DEPTH)
    ]
    for copy in loads + int_loads:
        copy.start()
    for g in range(chips):
        loads[g].wait()
        rows = slice(g * panel, (g + 1) * panel)
        for s in range(DEPTH):
            cols = slice(s * width, (s + 1) * width)
            a_hi[rows, cols], a_lo[rows, cols] = split(amps[g, s])
    height = occ * part
    dot = functools.partial(lax.dot_general, dimension_numbers=NT, preferred_element_type=jnp.float32)
    groups = [(h, c) for h in range(parts) for c in range(CORES)]
    blocks = height // BLOCK

    def cut(n, s):
        h, c = groups[n]
        rows, cols = slice(n * height, (n + 1) * height), slice(s * width, (s + 1) * width)
        i_hi[rows, cols], i_lo[rows, cols] = split(ints[h, c * DEPTH + s].reshape(height, width))

    for s in range(DEPTH):
        int_loads[s].wait()
        cut(0, s)
    for n, (h, c) in enumerate(groups):
        more = n + 1 < len(groups)
        for copy in int_loads[(n + 1) * DEPTH : (n + 2) * DEPTH] if more else []:
            copy.wait()
        for m in range(blocks):
            at = slice(n * height + m * BLOCK, n * height + (m + 1) * BLOCK)
            sums = dot(i_hi[at], a_lo[...]) + dot(i_lo[at], a_hi[...]) + dot(i_hi[at], a_hi[...])
            at = slice(c * occ + m * BLOCK // part, c * occ + (m + 1) * BLOCK // part)
            out[at, h * part : (h + 1) * part, :] = sums.reshape(BLOCK // part, part, chips * panel)
            for s in range(m * DEPTH // blocks, (m + 1) * DEPTH // blocks) if more else []:
                cut(n + 1, s)
    core = places[3]
    copies = [
        pltpu.make_async_copy(out, whole, out_sem.at[0]),
        pltpu.make_async_copy(out.at[pl.ds(core * occ, occ)], own_all, out_sem.at[1]),
        pltpu.make_async_copy(out.at[pl.ds((1 - core) * occ, occ)], other_all, out_sem.at[2]),
    ]
    for copy in copies:
        copy.start()
    for copy in copies:
        copy.wait()


def finish_kernel(dims, pieces, slots, places, panel_of, e_occ, e_b, e_vir, *refs):
    occ, panel, virtuals = dims
    out_hbm, slot_of, dir_v, mir_v, out_v, in_sem, out_sem = refs[3 * len(pieces) :]
    v, x, y, core = places[0], places[1], places[2], places[3]
    loads = []
    for j in range(occ):
        mine = []
        for n, (first, size, rows, height) in enumerate(pieces):
            own, other, mirror = refs[3 * n : 3 * n + 3]
            for e in range(CORES):
                at = (j, pl.ds(rows, height), pl.ds(e * virtuals // 2 + first, size))
                mine.append(((other if e else own).at[j], dir_v.at[at]))
                mine.append((mirror.at[lax.rem(core + e, CORES) * occ + j], mir_v.at[at]))
        loads.append([pltpu.make_async_copy(a, b, in_sem.at[j, n]) for n, (a, b) in enumerate(mine)])
        for copy in loads[j]:
            copy.start()
    for s, ((dx, dy), e) in enumerate(slots):
        chip = lax.rem(x + dx, SIDE) * SIDE + lax.rem(y + dy, SIDE)
        slot_of[panel_of[chip * CORES + lax.rem(core + e, CORES)]] = s
    lanes = 2 * panel
    lane = lax.broadcasted_iota(jnp.int32, (panel, lanes), 1)
    for j in range(occ):
        for copy in loads[j]:
            copy.wait()
        base = (e_occ[v] + e_occ[j]) - e_b[...]
        for t in range(virtuals // lanes):
            sides = []
            for h in range(2):
                s = slot_of[2 * t + h]
                cols = pl.ds(pl.multiple_of((s // 2) * lanes, lanes), lanes)
                diff = dir_v[j, :, cols] - mir_v[j, :, cols]
                sides.append(pltpu.roll(diff, lax.rem(s + h, 2) * panel, 1))
            cols = slice(t * lanes, (t + 1) * lanes)
            out_v[j, :, cols] = jnp.where(lane < panel, sides[0], sides[1]) / (base - e_vir[:, cols])
        pltpu.make_async_copy(out_v.at[j], out_hbm.at[j], out_sem.at[j]).start()
    for j in range(occ):
        pltpu.make_async_copy(out_v.at[j], out_hbm.at[j], out_sem.at[j]).wait()


def body(amps, ints, panel_of, e_occ, e_vir):
    occ, panel, width = amps.shape
    virtuals = e_vir.shape[0]
    f32, bf16 = jnp.float32, jnp.bfloat16
    index = [lax.axis_index(name).astype(jnp.int32) for name in ("virt", "x", "y", "core")]
    places = jnp.stack(index)
    part = panel // HALVES

    def move(data, dx, dy):
        name, step = ("x", dx) if dx else ("y", dy)
        return lax.ppermute(data, name, [(n, (n - step) % SIDE) for n in range(SIDE)])

    int_all = [lax.all_gather(ints[:, h * part : (h + 1) * part], ("core", "virt"), axis=0) for h in range(HALVES)]
    held = {(0, 0): lax.all_to_all(amps, "virt", split_axis=0, concat_axis=0, tiled=True)}
    sets = [[wrap(*chip) for chip in chips] for chips in SETS]
    starts = [sum(map(len, sets[:k])) * panel for k in range(len(sets))]

    def bring(routes, after=()):
        for to, (dx, dy) in routes:
            data = held[wrap(to[0] - dx, to[1] - dy)]
            if after:
                data = lax.optimization_barrier([data, *after])[0]
            held[wrap(*to)] = move(data, dx, dy)

    bring(FIRST)
    soon = [wrap(*chip) for chip in SOON]
    int_all[0], *ready = lax.optimization_barrier([int_all[0]] + [held[chip] for chip in soon])
    held.update(zip(soon, ready))

    arrays, places_of, mirror = [], [], []
    for n, (k, halves) in enumerate(PIECES):
        chips, parts = sets[k], len(halves)
        size, tall = len(chips) * panel, parts * part
        every = jax.ShapeDtypeStruct((occ, tall, size), f32)
        both = jax.ShapeDtypeStruct((CORES * occ, tall, size), f32)
        own_all, other_all, whole = pl.pallas_call(
            functools.partial(product_kernel, (occ, part, panel, width, parts, len(chips))),
            out_shape=[every, every, both],
            in_specs=[SMEM] + [ANY] * (parts + len(chips)),
            out_specs=[ANY] * 3,
            scratch_shapes=[
                pltpu.VMEM((parts, CORES * DEPTH, occ, part, width), f32),
                pltpu.VMEM((len(chips), DEPTH, panel, width), f32),
                pltpu.VMEM((CORES * occ * tall, DEPTH * width), bf16),
                pltpu.VMEM((CORES * occ * tall, DEPTH * width), bf16),
                pltpu.VMEM((size, DEPTH * width), bf16),
                pltpu.VMEM((size, DEPTH * width), bf16),
                pltpu.VMEM(both.shape, f32),
                pltpu.SemaphoreType.DMA((parts, CORES * DEPTH)),
                pltpu.SemaphoreType.DMA((len(chips),)),
                pltpu.SemaphoreType.DMA((3,)),
            ],
            compiler_params=LIMIT,
            cost_estimate=COSTS[n],
            name=f"product_{n}",
        )(places, *[int_all[h] for h in halves], *[held[chip] for chip in chips])
        if mirror:
            whole, mirror[-1] = lax.optimization_barrier((whole, mirror[-1]))
        mirror.append(lax.all_to_all(whole, ("core", "virt"), split_axis=0, concat_axis=0, tiled=True))
        arrays.append([own_all, lax.ppermute(other_all, "core", [(0, 1), (1, 0)])])
        places_of.append((starts[k], size, halves[0] * part, tall))
        if n + 1 < len(PIECES):
            int_all = list(lax.optimization_barrier(int_all + [own_all])[:HALVES])
            bring(LAST, [arrays[-1][1]])
    for n, (pair_of, back) in enumerate(zip(arrays, mirror)):
        pair_of.append(back)
        where = [pltpu.HBM, pltpu.HBM, pltpu.HBM if n + 1 < len(PIECES) else pltpu.VMEM]
        arrays[n] = [pltpu.with_memory_space_constraint(*both) for both in zip(pair_of, where)]

    slots = [(chip, e) for e in range(CORES) for chips in sets for chip in chips]
    pair = (index[1] * SIDE + index[2]) * CORES + index[3]
    e_b = lax.dynamic_slice(e_vir, (pair * panel,), (panel,)).reshape(panel, 1)
    out = pl.pallas_call(
        functools.partial(finish_kernel, (occ, panel, virtuals), places_of, slots),
        out_shape=jax.ShapeDtypeStruct((occ, panel, virtuals), f32),
        in_specs=[SMEM, SMEM, SMEM, VMEM, VMEM] + [HBM] * (3 * len(PIECES) - 1) + [VMEM],
        out_specs=ANY,
        scratch_shapes=[
            pltpu.SMEM((virtuals // panel,), jnp.int32),
            pltpu.VMEM((occ, panel, virtuals), f32),
            pltpu.VMEM((occ, panel, virtuals), f32),
            pltpu.VMEM((occ, panel, virtuals), f32),
            pltpu.SemaphoreType.DMA((occ, 2 * CORES * len(PIECES))),
            pltpu.SemaphoreType.DMA((occ,)),
        ],
        compiler_params=pltpu.CompilerParams(vmem_limit_bytes=48 * 2**20),
        name="finish",
    )(places, panel_of, e_occ, e_b, e_vir.reshape(1, virtuals), *[a for group in arrays for a in group])
    return out[None]


def solution(mesh):
    fine = Mesh(mesh.devices.reshape(SIDE, SIDE, CORES, DEPTH), ("x", "y", "core", "virt"))
    rows = ("x", "y", "core")
    in_specs = (P(None, rows, "virt"), P(None, rows, "virt"), P(), P(), P())
    out_specs = P("virt", None, rows, None)
    return jax.shard_map(body, mesh=fine, in_specs=in_specs, out_specs=out_specs, check_vma=False)
```

```python
import functools

import jax
import jax.numpy as jnp
from jax import lax
from jax.experimental import pallas as pl
from jax.experimental.pallas import tpu as pltpu
from jax.sharding import Mesh, PartitionSpec as P

SIDE = 4
CORES = 2
DEPTH = 8
BLOCK = 256
NT = (((1,), (1,)), ((), ()))
SMEM = pl.BlockSpec(memory_space=pltpu.SMEM)
ANY = pl.BlockSpec(memory_space=pl.ANY)
VMEM = pl.BlockSpec(memory_space=pltpu.VMEM)
COSTS = [pl.CostEstimate(flops=f * 10**9, transcendentals=0, bytes_accessed=f * 10**6) for f in (60, 8)]
FIRST = [
    ((1, 0), (1, 0)),
    ((-1, 0), (-1, 0)),
    ((0, 1), (0, 1)),
    ((0, -1), (0, -1)),
    ((1, 1), (1, 0)),
    ((-1, -1), (-1, 0)),
    ((-1, 1), (0, 1)),
    ((1, -1), (0, -1)),
    ((2, 0), (1, 0)),
    ((0, 2), (0, 1)),
    ((2, 1), (-1, 0)),
    ((1, 2), (0, -1)),
]
LAST = [((2, -1), (1, 0)), ((-1, 2), (0, -1)), ((2, 2), (0, 1))]
SETS = [
    [(0, 0), (1, 0), (-1, 0), (0, 1), (0, -1), (1, 1), (-1, -1), (-1, 1)],
    [(1, -1), (2, 0), (0, 2), (2, 1), (1, 2), (2, -1), (-1, 2), (2, 2)],
]
EARLY = [(1, -1), (2, 0)]


def wrap(x, y):
    return x % SIDE, y % SIDE


def split(x):
    high = x.astype(jnp.bfloat16)
    return high, (x - high.astype(jnp.float32)).astype(jnp.bfloat16)


def split_kernel(dims, *refs):
    panel, width, chips = dims
    amps_hbm = refs[:chips]
    a_hi, a_lo, amps, amp_sem = refs[chips:]
    loads = [pltpu.make_async_copy(amps_hbm[g], amps.at[g], amp_sem.at[g]) for g in range(chips)]
    for copy in loads:
        copy.start()
    for g in range(chips):
        loads[g].wait()
        rows = slice(g * panel, (g + 1) * panel)
        for s in range(DEPTH):
            cols = slice(s * width, (s + 1) * width)
            a_hi[rows, cols], a_lo[rows, cols] = split(amps[g, s])


def product_kernel(dims, ints_hbm, a_hi, a_lo, whole, ints, i_hi, i_lo, out, int_sem, out_sem):
    occ, panel, width = dims
    loads = [pltpu.make_async_copy(ints_hbm.at[s], ints.at[s], int_sem.at[s]) for s in range(CORES * DEPTH)]
    for copy in loads:
        copy.start()
    height = occ * panel
    blocks = height // BLOCK
    dot = functools.partial(lax.dot_general, dimension_numbers=NT, preferred_element_type=jnp.float32)

    def cut(c, s):
        rows, cols = slice(c * height, (c + 1) * height), slice(s * width, (s + 1) * width)
        i_hi[rows, cols], i_lo[rows, cols] = split(ints[c * DEPTH + s].reshape(height, width))

    for s in range(DEPTH):
        loads[s].wait()
        cut(0, s)
    for copy in loads[DEPTH:]:
        copy.wait()
    stores = []
    for c in range(CORES):
        for m in range(blocks):
            at = slice(c * height + m * BLOCK, c * height + (m + 1) * BLOCK)
            sums = dot(i_hi[at], a_lo[...]) + dot(i_lo[at], a_hi[...]) + dot(i_hi[at], a_hi[...])
            at = slice(at.start // panel, at.stop // panel)
            out[at] = sums.reshape(BLOCK // panel, panel, -1)
            stores.append(pltpu.make_async_copy(out.at[at], whole.at[at], out_sem.at[len(stores)]))
            stores[-1].start()
            for s in range(m * DEPTH // blocks, (m + 1) * DEPTH // blocks) if c == 0 else []:
                cut(1, s)
    for copy in stores:
        copy.wait()


def finish_kernel(dims, pieces, slots, places, panel_of, e_occ, e_b, e_vir, *refs):
    occ, panel, virtuals = dims
    out_hbm, slot_of, dir_v, mir_v, out_v, in_sem, out_sem = refs[3 * len(pieces) :]
    v, x, y, core = places[0], places[1], places[2], places[3]
    loads = []
    for j in range(occ):
        mine = []
        for n, (first, size) in enumerate(pieces):
            own, other, mirror = refs[3 * n : 3 * n + 3]
            for e in range(CORES):
                at = (j, slice(None), pl.ds(e * virtuals // 2 + first, size))
                mine.append(((other if e else own).at[core * occ + j], dir_v.at[at]))
                mine.append((mirror.at[lax.rem(core + e, CORES) * occ + j], mir_v.at[at]))
        loads.append([pltpu.make_async_copy(a, b, in_sem.at[j, n]) for n, (a, b) in enumerate(mine)])
        for copy in loads[j]:
            copy.start()
    for s, ((dx, dy), e) in enumerate(slots):
        chip = lax.rem(x + dx, SIDE) * SIDE + lax.rem(y + dy, SIDE)
        slot_of[panel_of[chip * CORES + lax.rem(core + e, CORES)]] = s
    lanes = 2 * panel
    lane = lax.broadcasted_iota(jnp.int32, (panel, lanes), 1)
    for j in range(occ):
        for copy in loads[j]:
            copy.wait()
        base = (e_occ[v] + e_occ[j]) - e_b[...]
        for t in range(virtuals // lanes):
            sides = []
            for h in range(2):
                s = slot_of[2 * t + h]
                cols = pl.ds(pl.multiple_of((s // 2) * lanes, lanes), lanes)
                diff = dir_v[j, :, cols] - mir_v[j, :, cols]
                sides.append(pltpu.roll(diff, lax.rem(s + h, 2) * panel, 1))
            cols = slice(t * lanes, (t + 1) * lanes)
            out_v[j, :, cols] = jnp.where(lane < panel, sides[0], sides[1]) / (base - e_vir[:, cols])
        pltpu.make_async_copy(out_v.at[j], out_hbm.at[j], out_sem.at[j]).start()
    for j in range(occ):
        pltpu.make_async_copy(out_v.at[j], out_hbm.at[j], out_sem.at[j]).wait()


def body(amps, ints, panel_of, e_occ, e_vir):
    occ, panel, width = amps.shape
    virtuals = e_vir.shape[0]
    f32, bf16 = jnp.float32, jnp.bfloat16
    index = [lax.axis_index(name).astype(jnp.int32) for name in ("virt", "x", "y", "core")]
    places = jnp.stack(index)

    def move(data, dx, dy):
        name, step = ("x", dx) if dx else ("y", dy)
        return lax.ppermute(data, name, [(n, (n - step) % SIDE) for n in range(SIDE)])

    int_all = lax.all_gather(ints, ("core", "virt"), axis=0)
    held = {(0, 0): lax.all_to_all(amps, "virt", split_axis=0, concat_axis=0, tiled=True)}
    sets = [[wrap(*chip) for chip in chips] for chips in SETS]
    starts = [sum(map(len, sets[:k])) * panel for k in range(len(sets))]

    def bring(routes, after=()):
        for to, (dx, dy) in routes:
            data = held[wrap(to[0] - dx, to[1] - dy)]
            if after:
                data = lax.optimization_barrier([data, *after])[0]
            held[wrap(*to)] = move(data, dx, dy)

    bring(FIRST)
    arrays, places_of = [], []
    for n, chips in enumerate(sets):
        size = len(chips) * panel
        height = occ * panel
        wide = jax.ShapeDtypeStruct((size, DEPTH * width), bf16)
        parts = pl.pallas_call(
            functools.partial(split_kernel, (panel, width, len(chips))),
            out_shape=[wide, wide],
            in_specs=[ANY] * len(chips),
            out_specs=[VMEM, VMEM],
            scratch_shapes=[
                pltpu.VMEM((len(chips), DEPTH, panel, width), f32),
                pltpu.SemaphoreType.DMA((len(chips),)),
            ],
            compiler_params=pltpu.CompilerParams(vmem_limit_bytes=24 * 2**20),
            cost_estimate=COSTS[n],
            name=f"split_{n}",
        )(*[pltpu.with_memory_space_constraint(held[chip], pltpu.HBM) for chip in chips])
        if n == 0:
            early = [held[wrap(*chip)] for chip in EARLY]
            int_all, *parts = lax.optimization_barrier([int_all, *parts, *early])[: 1 + len(parts)]
        parts = [pltpu.with_memory_space_constraint(part, pltpu.VMEM) for part in parts]
        both = pltpu.HBM((CORES * occ, panel, size), f32)
        whole = pl.pallas_call(
            functools.partial(product_kernel, (occ, panel, width)),
            out_shape=both,
            in_specs=[ANY, VMEM, VMEM],
            out_specs=ANY,
            scratch_shapes=[
                pltpu.VMEM((CORES * DEPTH, occ, panel, width), f32),
                pltpu.VMEM((CORES * height, DEPTH * width), bf16),
                pltpu.VMEM((CORES * height, DEPTH * width), bf16),
                pltpu.VMEM(both.shape, f32),
                pltpu.SemaphoreType.DMA((CORES * DEPTH,)),
                pltpu.SemaphoreType.DMA((CORES * height // BLOCK,)),
            ],
            compiler_params=pltpu.CompilerParams(vmem_limit_bytes=36 * 2**20),
            cost_estimate=COSTS[n],
            name=f"product_{n}",
        )(pltpu.with_memory_space_constraint(int_all, pltpu.HBM), *parts)
        sent = lax.optimization_barrier([whole, arrays[-1][2]])[0] if arrays else whole
        swapped = lax.ppermute(whole, "core", [(0, 1), (1, 0)])
        mirror = lax.all_to_all(sent, ("core", "virt"), split_axis=0, concat_axis=0, tiled=True)
        arrays.append([whole, swapped, mirror])
        places_of.append((starts[n], size))
        if n == 0:
            int_all = lax.optimization_barrier([int_all, whole])[0]
            bring(LAST, [swapped])
    where = [pltpu.HBM, pltpu.HBM, pltpu.VMEM]
    arrays = [[pltpu.with_memory_space_constraint(*both) for both in zip(group, where)] for group in arrays]

    slots = [(chip, e) for e in range(CORES) for chips in sets for chip in chips]
    pair = (index[1] * SIDE + index[2]) * CORES + index[3]
    e_b = lax.dynamic_slice(e_vir, (pair * panel,), (panel,)).reshape(panel, 1)
    out = pl.pallas_call(
        functools.partial(finish_kernel, (occ, panel, virtuals), places_of, slots),
        out_shape=jax.ShapeDtypeStruct((occ, panel, virtuals), f32),
        in_specs=[SMEM, SMEM, SMEM, VMEM, VMEM] + [ANY, ANY, VMEM] * len(sets),
        out_specs=ANY,
        scratch_shapes=[
            pltpu.SMEM((virtuals // panel,), jnp.int32),
            pltpu.VMEM((occ, panel, virtuals), f32),
            pltpu.VMEM((occ, panel, virtuals), f32),
            pltpu.VMEM((occ, panel, virtuals), f32),
            pltpu.SemaphoreType.DMA((occ, 2 * CORES * len(sets))),
            pltpu.SemaphoreType.DMA((occ,)),
        ],
        compiler_params=pltpu.CompilerParams(vmem_limit_bytes=48 * 2**20),
        name="finish",
    )(places, panel_of, e_occ, e_b, e_vir.reshape(1, virtuals), *[a for group in arrays for a in group])
    return out[None]


def solution(mesh):
    fine = Mesh(mesh.devices.reshape(SIDE, SIDE, CORES, DEPTH), ("x", "y", "core", "virt"))
    rows = ("x", "y", "core")
    in_specs = (P(None, rows, "virt"), P(None, rows, "virt"), P(), P(), P())
    out_specs = P("virt", None, rows, None)
    return jax.shard_map(body, mesh=fine, in_specs=in_specs, out_specs=out_specs, check_vma=False)
```

```python
import functools

import jax
import jax.numpy as jnp
from jax import lax
from jax.experimental import pallas as pl
from jax.experimental.pallas import tpu as pltpu
from jax.sharding import Mesh, PartitionSpec as P

SIDE = 4
CORES = 2
DEPTH = 8
BLOCK = 256
NT = (((1,), (1,)), ((), ()))
SMEM = pl.BlockSpec(memory_space=pltpu.SMEM)
ANY = pl.BlockSpec(memory_space=pl.ANY)
VMEM = pl.BlockSpec(memory_space=pltpu.VMEM)
COSTS = [pl.CostEstimate(flops=f * 10**9, transcendentals=0, bytes_accessed=f * 10**6) for f in (60, 8)]
FIRST = [
    ((1, 0), (1, 0)),
    ((-1, 0), (-1, 0)),
    ((0, 1), (0, 1)),
    ((0, -1), (0, -1)),
    ((1, 1), (1, 0)),
    ((-1, -1), (-1, 0)),
    ((-1, 1), (0, 1)),
    ((1, -1), (0, -1)),
    ((2, 0), (1, 0)),
    ((0, 2), (0, 1)),
    ((2, 1), (-1, 0)),
    ((1, 2), (0, -1)),
]
LAST = [((2, -1), (1, 0)), ((-1, 2), (0, -1)), ((2, 2), (0, 1))]
SETS = [
    [(0, 0), (1, 0), (-1, 0), (0, 1), (0, -1), (1, 1), (-1, -1), (-1, 1)],
    [(1, -1), (2, 0), (0, 2), (2, 1), (1, 2), (2, -1), (-1, 2), (2, 2)],
]
EARLY = [(1, -1), (2, 0)]


def wrap(x, y):
    return x % SIDE, y % SIDE


def split(x):
    high = x.astype(jnp.bfloat16)
    return high, (x - high.astype(jnp.float32)).astype(jnp.bfloat16)


def split_kernel(dims, *refs):
    panel, width, chips = dims
    amps_hbm = refs[:chips]
    a_hi, a_lo_hbm, amps, a_lo, amp_sem, out_sem = refs[chips:]
    loads = [pltpu.make_async_copy(amps_hbm[g], amps.at[g], amp_sem.at[g]) for g in range(chips)]
    for copy in loads:
        copy.start()
    for g in range(chips):
        loads[g].wait()
        rows = slice(g * panel, (g + 1) * panel)
        for s in range(DEPTH):
            cols = slice(s * width, (s + 1) * width)
            a_hi[rows, cols], a_lo[rows, cols] = split(amps[g, s])
    store = pltpu.make_async_copy(a_lo, a_lo_hbm, out_sem)
    store.start()
    store.wait()


def product_kernel(dims, ints_hbm, a_hi, a_lo_hbm, whole, a_lo, ints, i_hi, i_lo, out, a_sem, int_sem, out_sem):
    occ, panel, width = dims
    loads = [pltpu.make_async_copy(ints_hbm.at[s], ints.at[s], int_sem.at[s]) for s in range(CORES * DEPTH)]
    low = pltpu.make_async_copy(a_lo_hbm, a_lo, a_sem)
    for copy in loads[:DEPTH] + [low] + loads[DEPTH:]:
        copy.start()
    height = occ * panel
    blocks = height // BLOCK
    dot = functools.partial(lax.dot_general, dimension_numbers=NT, preferred_element_type=jnp.float32)

    def cut(c, s):
        rows, cols = slice(c * height, (c + 1) * height), slice(s * width, (s + 1) * width)
        i_hi[rows, cols], i_lo[rows, cols] = split(ints[c * DEPTH + s].reshape(height, width))

    for s in range(DEPTH):
        loads[s].wait()
        cut(0, s)
    for copy in [low] + loads[DEPTH:]:
        copy.wait()
    stores = []
    for c in range(CORES):
        for m in range(blocks):
            at = slice(c * height + m * BLOCK, c * height + (m + 1) * BLOCK)
            sums = dot(i_hi[at], a_lo[...]) + dot(i_lo[at], a_hi[...]) + dot(i_hi[at], a_hi[...])
            at = slice(at.start // panel, at.stop // panel)
            out[at] = sums.reshape(BLOCK // panel, panel, -1)
            stores.append(pltpu.make_async_copy(out.at[at], whole.at[at], out_sem.at[len(stores)]))
            stores[-1].start()
            for s in range(m * DEPTH // blocks, (m + 1) * DEPTH // blocks) if c == 0 else []:
                cut(1, s)
    for copy in stores:
        copy.wait()


def finish_kernel(dims, pieces, slots, places, panel_of, e_occ, e_b, e_vir, *refs):
    occ, panel, virtuals = dims
    out_hbm, slot_of, dir_v, mir_v, out_v, in_sem, out_sem = refs[3 * len(pieces) :]
    v, x, y, core = places[0], places[1], places[2], places[3]
    loads = []
    for j in range(occ):
        mine = []
        for n, (first, size) in enumerate(pieces):
            own, other, mirror = refs[3 * n : 3 * n + 3]
            for e in range(CORES):
                at = (j, slice(None), pl.ds(e * virtuals // 2 + first, size))
                mine.append(((other if e else own).at[core * occ + j], dir_v.at[at]))
                mine.append((mirror.at[lax.rem(core + e, CORES) * occ + j], mir_v.at[at]))
        loads.append([pltpu.make_async_copy(a, b, in_sem.at[j, n]) for n, (a, b) in enumerate(mine)])
        for copy in loads[j]:
            copy.start()
    for s, ((dx, dy), e) in enumerate(slots):
        chip = lax.rem(x + dx, SIDE) * SIDE + lax.rem(y + dy, SIDE)
        slot_of[panel_of[chip * CORES + lax.rem(core + e, CORES)]] = s
    lanes = 2 * panel
    lane = lax.broadcasted_iota(jnp.int32, (panel, lanes), 1)
    for j in range(occ):
        for copy in loads[j]:
            copy.wait()
        base = (e_occ[v] + e_occ[j]) - e_b[...]
        for t in range(virtuals // lanes):
            sides = []
            for h in range(2):
                s = slot_of[2 * t + h]
                cols = pl.ds(pl.multiple_of((s // 2) * lanes, lanes), lanes)
                diff = dir_v[j, :, cols] - mir_v[j, :, cols]
                sides.append(pltpu.roll(diff, lax.rem(s + h, 2) * panel, 1))
            cols = slice(t * lanes, (t + 1) * lanes)
            out_v[j, :, cols] = jnp.where(lane < panel, sides[0], sides[1]) / (base - e_vir[:, cols])
        pltpu.make_async_copy(out_v.at[j], out_hbm.at[j], out_sem.at[j]).start()
    for j in range(occ):
        pltpu.make_async_copy(out_v.at[j], out_hbm.at[j], out_sem.at[j]).wait()


def body(amps, ints, panel_of, e_occ, e_vir):
    occ, panel, width = amps.shape
    virtuals = e_vir.shape[0]
    f32, bf16 = jnp.float32, jnp.bfloat16
    index = [lax.axis_index(name).astype(jnp.int32) for name in ("virt", "x", "y", "core")]
    places = jnp.stack(index)

    def move(data, dx, dy):
        name, step = ("x", dx) if dx else ("y", dy)
        return lax.ppermute(data, name, [(n, (n - step) % SIDE) for n in range(SIDE)])

    int_all = lax.all_gather(ints, ("core", "virt"), axis=0)
    held = {(0, 0): lax.all_to_all(amps, "virt", split_axis=0, concat_axis=0, tiled=True)}
    sets = [[wrap(*chip) for chip in chips] for chips in SETS]
    starts = [sum(map(len, sets[:k])) * panel for k in range(len(sets))]

    def bring(routes, after=()):
        for to, (dx, dy) in routes:
            data = held[wrap(to[0] - dx, to[1] - dy)]
            if after:
                data = lax.optimization_barrier([data, *after])[0]
            held[wrap(*to)] = move(data, dx, dy)

    bring(FIRST)
    arrays, places_of = [], []
    for n, chips in enumerate(sets):
        size = len(chips) * panel
        height = occ * panel
        wide = jax.ShapeDtypeStruct((size, DEPTH * width), bf16)
        parts = pl.pallas_call(
            functools.partial(split_kernel, (panel, width, len(chips))),
            out_shape=[wide, pltpu.HBM(wide.shape, bf16)],
            in_specs=[ANY] * len(chips),
            out_specs=[VMEM, ANY],
            scratch_shapes=[
                pltpu.VMEM((len(chips), DEPTH, panel, width), f32),
                pltpu.VMEM(wide.shape, bf16),
                pltpu.SemaphoreType.DMA((len(chips),)),
                pltpu.SemaphoreType.DMA,
            ],
            compiler_params=pltpu.CompilerParams(vmem_limit_bytes=8 * 2**20),
            cost_estimate=COSTS[n],
            name=f"split_{n}",
        )(*[pltpu.with_memory_space_constraint(held[chip], pltpu.HBM) for chip in chips])
        if n == 0:
            early = [held[wrap(*chip)] for chip in EARLY]
            int_all, *parts = lax.optimization_barrier([int_all, *parts, *early])[: 1 + len(parts)]
        parts = [pltpu.with_memory_space_constraint(*both) for both in zip(parts, [pltpu.VMEM, pltpu.HBM])]
        both = pltpu.HBM((CORES * occ, panel, size), f32)
        whole = pl.pallas_call(
            functools.partial(product_kernel, (occ, panel, width)),
            out_shape=both,
            in_specs=[ANY, VMEM, ANY],
            out_specs=ANY,
            scratch_shapes=[
                pltpu.VMEM(wide.shape, bf16),
                pltpu.VMEM((CORES * DEPTH, occ, panel, width), f32),
                pltpu.VMEM((CORES * height, DEPTH * width), bf16),
                pltpu.VMEM((CORES * height, DEPTH * width), bf16),
                pltpu.VMEM(both.shape, f32),
                pltpu.SemaphoreType.DMA,
                pltpu.SemaphoreType.DMA((CORES * DEPTH,)),
                pltpu.SemaphoreType.DMA((CORES * height // BLOCK,)),
            ],
            compiler_params=pltpu.CompilerParams(vmem_limit_bytes=24 * 2**20),
            cost_estimate=COSTS[n],
            name=f"product_{n}",
        )(pltpu.with_memory_space_constraint(int_all, pltpu.HBM), *parts)
        sent = lax.optimization_barrier([whole, arrays[-1][2]])[0] if arrays else whole
        swapped = lax.ppermute(whole, "core", [(0, 1), (1, 0)])
        mirror = lax.all_to_all(sent, ("core", "virt"), split_axis=0, concat_axis=0, tiled=True)
        arrays.append([whole, swapped, mirror])
        places_of.append((starts[n], size))
        if n == 0:
            int_all = lax.optimization_barrier([int_all, whole])[0]
            bring(LAST, [swapped])
    fixed = lambda array, place: array if place is None else pltpu.with_memory_space_constraint(array, place)
    where = [[pltpu.HBM, pltpu.HBM, pltpu.VMEM], [pltpu.HBM, pltpu.HBM, None]]
    arrays = [[fixed(*both) for both in zip(*groups)] for groups in zip(arrays, where)]

    slots = [(chip, e) for e in range(CORES) for chips in sets for chip in chips]
    pair = (index[1] * SIDE + index[2]) * CORES + index[3]
    e_b = lax.dynamic_slice(e_vir, (pair * panel,), (panel,)).reshape(panel, 1)
    out = pl.pallas_call(
        functools.partial(finish_kernel, (occ, panel, virtuals), places_of, slots),
        out_shape=jax.ShapeDtypeStruct((occ, panel, virtuals), f32),
        in_specs=[SMEM, SMEM, SMEM, VMEM, VMEM] + [ANY, ANY, VMEM, ANY, ANY, ANY],
        out_specs=ANY,
        scratch_shapes=[
            pltpu.SMEM((virtuals // panel,), jnp.int32),
            pltpu.VMEM((occ, panel, virtuals), f32),
            pltpu.VMEM((occ, panel, virtuals), f32),
            pltpu.VMEM((occ, panel, virtuals), f32),
            pltpu.SemaphoreType.DMA((occ, 2 * CORES * len(sets))),
            pltpu.SemaphoreType.DMA((occ,)),
        ],
        compiler_params=pltpu.CompilerParams(vmem_limit_bytes=16 * 2**20),
        name="finish",
    )(places, panel_of, e_occ, e_b, e_vir.reshape(1, virtuals), *[a for group in arrays for a in group])
    return out[None]


def solution(mesh):
    fine = Mesh(mesh.devices.reshape(SIDE, SIDE, CORES, DEPTH), ("x", "y", "core", "virt"))
    rows = ("x", "y", "core")
    in_specs = (P(None, rows, "virt"), P(None, rows, "virt"), P(), P(), P())
    out_specs = P("virt", None, rows, None)
    return jax.shard_map(body, mesh=fine, in_specs=in_specs, out_specs=out_specs, check_vma=False)
```

```python
import functools

import jax
import jax.numpy as jnp
from jax import lax
from jax.experimental import pallas as pl
from jax.experimental.pallas import tpu as pltpu
from jax.sharding import Mesh, PartitionSpec as P

SIDE = 4
CORES = 2
DEPTH = 8
BLOCK = 256
NT = (((1,), (1,)), ((), ()))
SMEM = pl.BlockSpec(memory_space=pltpu.SMEM)
ANY = pl.BlockSpec(memory_space=pl.ANY)
VMEM = pl.BlockSpec(memory_space=pltpu.VMEM)
COSTS = [pl.CostEstimate(flops=f * 10**9, transcendentals=0, bytes_accessed=f * 10**6) for f in (60, 8)]
FIRST = [
    ((1, 0), (1, 0)),
    ((-1, 0), (-1, 0)),
    ((0, 1), (0, 1)),
    ((0, -1), (0, -1)),
    ((1, 1), (1, 0)),
    ((-1, -1), (-1, 0)),
    ((-1, 1), (0, 1)),
    ((1, -1), (0, -1)),
    ((2, 0), (1, 0)),
    ((0, 2), (0, 1)),
    ((2, 1), (-1, 0)),
    ((1, 2), (0, -1)),
]
LAST = [((2, -1), (1, 0)), ((-1, 2), (0, -1)), ((2, 2), (0, 1))]
SETS = [
    [(0, 0), (1, 0), (-1, 0), (0, 1), (0, -1), (1, 1), (-1, -1), (-1, 1)],
    [(1, -1), (2, 0), (0, 2), (2, 1), (1, 2), (2, -1), (-1, 2), (2, 2)],
]
EARLY = [(1, -1), (2, 0)]


def wrap(x, y):
    return x % SIDE, y % SIDE


def split(x):
    high = x.astype(jnp.bfloat16)
    return high, (x - high.astype(jnp.float32)).astype(jnp.bfloat16)


def split_kernel(dims, *refs):
    panel, width, chips = dims
    amps_hbm = refs[:chips]
    a_hi, a_lo_hbm, amps, a_lo, amp_sem, out_sem = refs[chips:]
    loads = [pltpu.make_async_copy(amps_hbm[g], amps.at[g], amp_sem.at[g]) for g in range(chips)]
    for copy in loads:
        copy.start()
    for g in range(chips):
        loads[g].wait()
        rows = slice(g * panel, (g + 1) * panel)
        for s in range(DEPTH):
            cols = slice(s * width, (s + 1) * width)
            a_hi[rows, cols], a_lo[rows, cols] = split(amps[g, s])
    store = pltpu.make_async_copy(a_lo, a_lo_hbm, out_sem)
    store.start()
    store.wait()


def product_kernel(dims, ints_hbm, a_hi, a_lo_hbm, whole, a_lo, ints, i_hi, i_lo, out, a_sem, int_sem, out_sem):
    occ, panel, width = dims
    loads = [pltpu.make_async_copy(ints_hbm.at[s], ints.at[s], int_sem.at[s]) for s in range(CORES * DEPTH)]
    low = pltpu.make_async_copy(a_lo_hbm, a_lo, a_sem)
    for copy in loads[:DEPTH] + [low] + loads[DEPTH:]:
        copy.start()
    height = occ * panel
    blocks = height // BLOCK
    dot = functools.partial(lax.dot_general, dimension_numbers=NT, preferred_element_type=jnp.float32)

    def cut(c, s):
        rows, cols = slice(c * height, (c + 1) * height), slice(s * width, (s + 1) * width)
        i_hi[rows, cols], i_lo[rows, cols] = split(ints[c * DEPTH + s].reshape(height, width))

    for s in range(DEPTH):
        loads[s].wait()
        cut(0, s)
    for copy in [low] + loads[DEPTH:]:
        copy.wait()
    stores = []
    for c in range(CORES):
        for m in range(blocks):
            at = slice(c * height + m * BLOCK, c * height + (m + 1) * BLOCK)
            sums = dot(i_hi[at], a_lo[...]) + dot(i_lo[at], a_hi[...]) + dot(i_hi[at], a_hi[...])
            at = slice(at.start // panel, at.stop // panel)
            out[at] = sums.reshape(BLOCK // panel, panel, -1)
            stores.append(pltpu.make_async_copy(out.at[at], whole.at[at], out_sem.at[len(stores)]))
            stores[-1].start()
            for s in range(m * DEPTH // blocks, (m + 1) * DEPTH // blocks) if c == 0 else []:
                cut(1, s)
    for copy in stores:
        copy.wait()


def find_slots(slot_of, slots, places, panel_of):
    x, y, core = places[1], places[2], places[3]
    for s, ((dx, dy), e) in enumerate(slots):
        chip = lax.rem(x + dx, SIDE) * SIDE + lax.rem(y + dy, SIDE)
        slot_of[panel_of[chip * CORES + lax.rem(core + e, CORES)]] = s


def pick(data, j, t, slot_of, panel):
    lanes = 2 * panel
    lane = lax.broadcasted_iota(jnp.int32, (panel, lanes), 1)
    sides = []
    for h in range(2):
        s = slot_of[2 * t + h]
        cols = pl.ds(pl.multiple_of((s // 2) * lanes, lanes), lanes)
        sides.append(pltpu.roll(data(j, cols), lax.rem(s + h, 2) * panel, 1))
    return jnp.where(lane < panel, sides[0], sides[1])


def clear(block, columns):
    for first, size in columns:
        block[:, :, first : first + size] = jnp.zeros(block.shape[:2] + (size,), block.dtype)


def place_kernel(dims, slots, places, panel_of, own_0, other_0, mirror_0, own_1, other_1, placed_hbm, slot_of, dir_v, mir_v, placed, in_sem, out_sem):
    occ, panel, virtuals, pieces = dims
    core = places[3]
    loads = []
    for j in range(occ):
        mine = []
        for e in range(CORES):
            for (first, size), direct in zip(pieces, ((own_0, other_0), (own_1, other_1))):
                at = (j, slice(None), pl.ds(e * virtuals // 2 + first, size))
                mine.append((direct[e].at[core * occ + j], dir_v.at[at]))
            first, size = pieces[0]
            at = (j, slice(None), pl.ds(e * virtuals // 2 + first, size))
            mine.append((mirror_0.at[lax.rem(core + e, CORES) * occ + j], mir_v.at[at]))
        loads.append([pltpu.make_async_copy(a, b, in_sem.at[j, n]) for n, (a, b) in enumerate(mine)])
        for copy in loads[j]:
            copy.start()
    find_slots(slot_of, slots, places, panel_of)
    first, size = pieces[1]
    clear(mir_v, [(e * virtuals // 2 + first, size) for e in range(CORES)])
    for j in range(occ):
        for copy in loads[j]:
            copy.wait()
        for t in range(virtuals // (2 * panel)):
            part = pick(lambda j, cols: dir_v[j, :, cols] - mir_v[j, :, cols], j, t, slot_of, panel)
            placed[j, :, t * 2 * panel : (t + 1) * 2 * panel] = part
        pltpu.make_async_copy(placed.at[j], placed_hbm.at[j], out_sem.at[j]).start()
    for j in range(occ):
        pltpu.make_async_copy(placed.at[j], placed_hbm.at[j], out_sem.at[j]).wait()


def finish_kernel(dims, slots, places, panel_of, e_occ, e_b, e_vir, placed_hbm, mirror_1, out_hbm, slot_of, mir_v, placed, out_v, in_sem, out_sem):
    occ, panel, virtuals, pieces = dims
    v, core = places[0], places[3]
    first, size = pieces[1]
    loads = []
    for j in range(occ):
        for e in range(CORES):
            at = (j, slice(None), pl.ds(e * virtuals // 2 + first, size))
            source = mirror_1.at[lax.rem(core + e, CORES) * occ + j]
            loads.append(pltpu.make_async_copy(source, mir_v.at[at], in_sem.at[j, e]))
        loads.append(pltpu.make_async_copy(placed_hbm.at[j], placed.at[j], in_sem.at[j, CORES]))
    for copy in loads:
        copy.start()
    find_slots(slot_of, slots, places, panel_of)
    first, size = pieces[0]
    clear(mir_v, [(e * virtuals // 2 + first, size) for e in range(CORES)])
    for j in range(occ):
        for copy in loads[(CORES + 1) * j : (CORES + 1) * (j + 1)]:
            copy.wait()
        base = (e_occ[v] + e_occ[j]) - e_b[...]
        for t in range(virtuals // (2 * panel)):
            cols = slice(t * 2 * panel, (t + 1) * 2 * panel)
            part = pick(lambda j, cols: mir_v[j, :, cols], j, t, slot_of, panel)
            out_v[j, :, cols] = (placed[j, :, cols] - part) / (base - e_vir[:, cols])
        pltpu.make_async_copy(out_v.at[j], out_hbm.at[j], out_sem.at[j]).start()
    for j in range(occ):
        pltpu.make_async_copy(out_v.at[j], out_hbm.at[j], out_sem.at[j]).wait()


def body(amps, ints, panel_of, e_occ, e_vir):
    occ, panel, width = amps.shape
    virtuals = e_vir.shape[0]
    f32, bf16 = jnp.float32, jnp.bfloat16
    index = [lax.axis_index(name).astype(jnp.int32) for name in ("virt", "x", "y", "core")]
    places = jnp.stack(index)

    def move(data, dx, dy):
        name, step = ("x", dx) if dx else ("y", dy)
        return lax.ppermute(data, name, [(n, (n - step) % SIDE) for n in range(SIDE)])

    int_all = lax.all_gather(ints, ("core", "virt"), axis=0)
    held = {(0, 0): lax.all_to_all(amps, "virt", split_axis=0, concat_axis=0, tiled=True)}
    sets = [[wrap(*chip) for chip in chips] for chips in SETS]
    starts = [sum(map(len, sets[:k])) * panel for k in range(len(sets))]

    def bring(routes, after=()):
        for to, (dx, dy) in routes:
            data = held[wrap(to[0] - dx, to[1] - dy)]
            if after:
                data = lax.optimization_barrier([data, *after])[0]
            held[wrap(*to)] = move(data, dx, dy)

    bring(FIRST)
    arrays, places_of = [], []
    for n, chips in enumerate(sets):
        size = len(chips) * panel
        height = occ * panel
        wide = jax.ShapeDtypeStruct((size, DEPTH * width), bf16)
        parts = pl.pallas_call(
            functools.partial(split_kernel, (panel, width, len(chips))),
            out_shape=[wide, pltpu.HBM(wide.shape, bf16)],
            in_specs=[ANY] * len(chips),
            out_specs=[VMEM, ANY],
            scratch_shapes=[
                pltpu.VMEM((len(chips), DEPTH, panel, width), f32),
                pltpu.VMEM(wide.shape, bf16),
                pltpu.SemaphoreType.DMA((len(chips),)),
                pltpu.SemaphoreType.DMA,
            ],
            compiler_params=pltpu.CompilerParams(vmem_limit_bytes=8 * 2**20),
            cost_estimate=COSTS[n],
            name=f"split_{n}",
        )(*[pltpu.with_memory_space_constraint(held[chip], pltpu.HBM) for chip in chips])
        if n == 0:
            early = [held[wrap(*chip)] for chip in EARLY]
            int_all, *parts = lax.optimization_barrier([int_all, *parts, *early])[: 1 + len(parts)]
        parts = [pltpu.with_memory_space_constraint(*both) for both in zip(parts, [pltpu.VMEM, pltpu.HBM])]
        both = pltpu.HBM((CORES * occ, panel, size), f32)
        whole = pl.pallas_call(
            functools.partial(product_kernel, (occ, panel, width)),
            out_shape=both,
            in_specs=[ANY, VMEM, ANY],
            out_specs=ANY,
            scratch_shapes=[
                pltpu.VMEM(wide.shape, bf16),
                pltpu.VMEM((CORES * DEPTH, occ, panel, width), f32),
                pltpu.VMEM((CORES * height, DEPTH * width), bf16),
                pltpu.VMEM((CORES * height, DEPTH * width), bf16),
                pltpu.VMEM(both.shape, f32),
                pltpu.SemaphoreType.DMA,
                pltpu.SemaphoreType.DMA((CORES * DEPTH,)),
                pltpu.SemaphoreType.DMA((CORES * height // BLOCK,)),
            ],
            compiler_params=pltpu.CompilerParams(vmem_limit_bytes=24 * 2**20),
            cost_estimate=COSTS[n],
            name=f"product_{n}",
        )(pltpu.with_memory_space_constraint(int_all, pltpu.HBM), *parts)
        sent = lax.optimization_barrier([whole, arrays[-1][2]])[0] if arrays else whole
        swapped = lax.ppermute(whole, "core", [(0, 1), (1, 0)])
        mirror = lax.all_to_all(sent, ("core", "virt"), split_axis=0, concat_axis=0, tiled=True)
        arrays.append([whole, swapped, mirror])
        places_of.append((starts[n], size))
        if n == 0:
            int_all = lax.optimization_barrier([int_all, whole])[0]
            bring(LAST, [whole])
    slots = [(chip, e) for e in range(CORES) for chips in sets for chip in chips]
    pair = (index[1] * SIDE + index[2]) * CORES + index[3]
    e_b = lax.dynamic_slice(e_vir, (pair * panel,), (panel,)).reshape(panel, 1)
    dims = (occ, panel, virtuals, tuple(places_of))
    block = pltpu.VMEM((occ, panel, virtuals), f32)
    table = pltpu.SMEM((virtuals // panel,), jnp.int32)
    (own_0, other_0, mirror_0), (own_1, other_1, mirror_1) = arrays
    hbm = lambda array: pltpu.with_memory_space_constraint(array, pltpu.HBM)
    placed = pl.pallas_call(
        functools.partial(place_kernel, dims, slots),
        out_shape=pltpu.HBM((occ, panel, virtuals), f32),
        in_specs=[SMEM, SMEM, ANY, ANY, VMEM, ANY, ANY],
        out_specs=ANY,
        scratch_shapes=[table, block, block, block, pltpu.SemaphoreType.DMA((occ, 3 * CORES)), pltpu.SemaphoreType.DMA((occ,))],
        compiler_params=pltpu.CompilerParams(vmem_limit_bytes=16 * 2**20),
        name="place",
    )(places, panel_of, hbm(own_0), hbm(other_0), mirror_0, hbm(own_1), hbm(other_1))
    out = pl.pallas_call(
        functools.partial(finish_kernel, dims, slots),
        out_shape=jax.ShapeDtypeStruct((occ, panel, virtuals), f32),
        in_specs=[SMEM, SMEM, SMEM, VMEM, VMEM, ANY, ANY],
        out_specs=ANY,
        scratch_shapes=[table, block, block, block, pltpu.SemaphoreType.DMA((occ, CORES + 1)), pltpu.SemaphoreType.DMA((occ,))],
        compiler_params=pltpu.CompilerParams(vmem_limit_bytes=16 * 2**20),
        name="finish",
    )(places, panel_of, e_occ, e_b, e_vir.reshape(1, virtuals), hbm(placed), mirror_1)
    return out[None]


def solution(mesh):
    fine = Mesh(mesh.devices.reshape(SIDE, SIDE, CORES, DEPTH), ("x", "y", "core", "virt"))
    rows = ("x", "y", "core")
    in_specs = (P(None, rows, "virt"), P(None, rows, "virt"), P(), P(), P())
    out_specs = P("virt", None, rows, None)
    return jax.shard_map(body, mesh=fine, in_specs=in_specs, out_specs=out_specs, check_vma=False)
```

```python
import functools

import jax
import jax.numpy as jnp
from jax import lax
from jax.experimental import pallas as pl
from jax.experimental.pallas import tpu as pltpu
from jax.sharding import Mesh, PartitionSpec as P

SIDE = 4
CORES = 2
DEPTH = 8
BLOCK = 256
NT = (((1,), (1,)), ((), ()))
SMEM = pl.BlockSpec(memory_space=pltpu.SMEM)
ANY = pl.BlockSpec(memory_space=pl.ANY)
VMEM = pl.BlockSpec(memory_space=pltpu.VMEM)
COSTS = [pl.CostEstimate(flops=f * 10**9, transcendentals=0, bytes_accessed=f * 10**6) for f in (60, 8)]
FIRST = [
    ((1, 0), (1, 0)),
    ((-1, 0), (-1, 0)),
    ((0, 1), (0, 1)),
    ((0, -1), (0, -1)),
    ((1, 1), (1, 0)),
    ((-1, -1), (-1, 0)),
    ((-1, 1), (0, 1)),
    ((1, -1), (0, -1)),
    ((2, 0), (1, 0)),
    ((0, 2), (0, 1)),
    ((2, 1), (-1, 0)),
    ((1, 2), (0, -1)),
]
LAST = [((2, -1), (1, 0)), ((-1, 2), (0, -1)), ((2, 2), (0, 2))]
SETS = [
    [(0, 0), (1, 0), (-1, 0), (0, 1), (0, -1), (1, 1), (-1, -1), (-1, 1)],
    [(1, -1), (2, 0), (0, 2), (2, 1), (1, 2), (2, -1), (-1, 2), (2, 2)],
]
EARLY = [(1, -1), (2, 0)]


def wrap(x, y):
    return x % SIDE, y % SIDE


def split(x):
    high = x.astype(jnp.bfloat16)
    return high, (x - high.astype(jnp.float32)).astype(jnp.bfloat16)


def split_kernel(dims, *refs):
    panel, width, chips = dims
    amps_hbm = refs[:chips]
    a_hi, a_lo_hbm, amps, a_lo, amp_sem, out_sem = refs[chips:]
    loads = [pltpu.make_async_copy(amps_hbm[g], amps.at[g], amp_sem.at[g]) for g in range(chips)]
    for copy in loads:
        copy.start()
    for g in range(chips):
        loads[g].wait()
        rows = slice(g * panel, (g + 1) * panel)
        for s in range(DEPTH):
            cols = slice(s * width, (s + 1) * width)
            a_hi[rows, cols], a_lo[rows, cols] = split(amps[g, s])
    store = pltpu.make_async_copy(a_lo, a_lo_hbm, out_sem)
    store.start()
    store.wait()


def product_kernel(dims, ints_hbm, a_hi, a_lo_hbm, whole, a_lo, ints, i_hi, i_lo, out, a_sem, int_sem, out_sem):
    occ, panel, width = dims
    loads = [pltpu.make_async_copy(ints_hbm.at[s], ints.at[s], int_sem.at[s]) for s in range(CORES * DEPTH)]
    low = pltpu.make_async_copy(a_lo_hbm, a_lo, a_sem)
    for copy in loads[:DEPTH] + [low] + loads[DEPTH:]:
        copy.start()
    height = occ * panel
    blocks = height // BLOCK
    dot = functools.partial(lax.dot_general, dimension_numbers=NT, preferred_element_type=jnp.float32)

    def cut(c, s):
        rows, cols = slice(c * height, (c + 1) * height), slice(s * width, (s + 1) * width)
        i_hi[rows, cols], i_lo[rows, cols] = split(ints[c * DEPTH + s].reshape(height, width))

    for s in range(DEPTH):
        loads[s].wait()
        cut(0, s)
    for copy in [low] + loads[DEPTH:]:
        copy.wait()
    stores = []
    for c in range(CORES):
        for m in range(blocks):
            at = slice(c * height + m * BLOCK, c * height + (m + 1) * BLOCK)
            sums = dot(i_hi[at], a_lo[...]) + dot(i_lo[at], a_hi[...]) + dot(i_hi[at], a_hi[...])
            at = slice(at.start // panel, at.stop // panel)
            out[at] = sums.reshape(BLOCK // panel, panel, -1)
            stores.append(pltpu.make_async_copy(out.at[at], whole.at[at], out_sem.at[len(stores)]))
            stores[-1].start()
            for s in range(m * DEPTH // blocks, (m + 1) * DEPTH // blocks) if c == 0 else []:
                cut(1, s)
    for copy in stores:
        copy.wait()


def finish_kernel(dims, pieces, slots, places, panel_of, e_occ, e_b, e_vir, *refs):
    occ, panel, virtuals = dims
    out_hbm, slot_of, dir_v, mir_v, out_v, in_sem, out_sem = refs[3 * len(pieces) :]
    v, x, y, core = places[0], places[1], places[2], places[3]
    loads = []
    for j in range(occ):
        mine = []
        for n, (first, size) in enumerate(pieces):
            own, other, mirror = refs[3 * n : 3 * n + 3]
            for e in range(CORES):
                at = (j, slice(None), pl.ds(e * virtuals // 2 + first, size))
                mine.append(((other if e else own).at[core * occ + j], dir_v.at[at]))
                mine.append((mirror.at[lax.rem(core + e, CORES) * occ + j], mir_v.at[at]))
        loads.append([pltpu.make_async_copy(a, b, in_sem.at[j, n]) for n, (a, b) in enumerate(mine)])
        for copy in loads[j]:
            copy.start()
    for s, ((dx, dy), e) in enumerate(slots):
        chip = lax.rem(x + dx, SIDE) * SIDE + lax.rem(y + dy, SIDE)
        slot_of[panel_of[chip * CORES + lax.rem(core + e, CORES)]] = s
    lanes = 2 * panel
    lane = lax.broadcasted_iota(jnp.int32, (panel, lanes), 1)
    for j in range(occ):
        for copy in loads[j]:
            copy.wait()
        base = (e_occ[v] + e_occ[j]) - e_b[...]
        for t in range(virtuals // lanes):
            sides = []
            for h in range(2):
                s = slot_of[2 * t + h]
                cols = pl.ds(pl.multiple_of((s // 2) * lanes, lanes), lanes)
                diff = dir_v[j, :, cols] - mir_v[j, :, cols]
                sides.append(pltpu.roll(diff, lax.rem(s + h, 2) * panel, 1))
            cols = slice(t * lanes, (t + 1) * lanes)
            out_v[j, :, cols] = jnp.where(lane < panel, sides[0], sides[1]) / (base - e_vir[:, cols])
        pltpu.make_async_copy(out_v.at[j], out_hbm.at[j], out_sem.at[j]).start()
    for j in range(occ):
        pltpu.make_async_copy(out_v.at[j], out_hbm.at[j], out_sem.at[j]).wait()


def body(amps, ints, panel_of, e_occ, e_vir):
    occ, panel, width = amps.shape
    virtuals = e_vir.shape[0]
    f32, bf16 = jnp.float32, jnp.bfloat16
    index = [lax.axis_index(name).astype(jnp.int32) for name in ("virt", "x", "y", "core")]
    places = jnp.stack(index)

    def move(data, dx, dy):
        name, step = ("x", dx) if dx else ("y", dy)
        return lax.ppermute(data, name, [(n, (n - step) % SIDE) for n in range(SIDE)])

    int_all = lax.all_gather(ints, ("core", "virt"), axis=0)
    held = {(0, 0): lax.all_to_all(amps, "virt", split_axis=0, concat_axis=0, tiled=True)}
    sets = [[wrap(*chip) for chip in chips] for chips in SETS]
    starts = [sum(map(len, sets[:k])) * panel for k in range(len(sets))]

    def bring(routes, after=()):
        for to, (dx, dy) in routes:
            data = held[wrap(to[0] - dx, to[1] - dy)]
            if after:
                data = lax.optimization_barrier([data, *after])[0]
            held[wrap(*to)] = move(data, dx, dy)

    bring(FIRST)
    arrays, places_of = [], []
    for n, chips in enumerate(sets):
        size = len(chips) * panel
        height = occ * panel
        wide = jax.ShapeDtypeStruct((size, DEPTH * width), bf16)
        parts = pl.pallas_call(
            functools.partial(split_kernel, (panel, width, len(chips))),
            out_shape=[wide, pltpu.HBM(wide.shape, bf16)],
            in_specs=[ANY] * len(chips),
            out_specs=[VMEM, ANY],
            scratch_shapes=[
                pltpu.VMEM((len(chips), DEPTH, panel, width), f32),
                pltpu.VMEM(wide.shape, bf16),
                pltpu.SemaphoreType.DMA((len(chips),)),
                pltpu.SemaphoreType.DMA,
            ],
            compiler_params=pltpu.CompilerParams(vmem_limit_bytes=8 * 2**20),
            cost_estimate=COSTS[n],
            name=f"split_{n}",
        )(*[pltpu.with_memory_space_constraint(held[chip], pltpu.HBM) for chip in chips])
        if n == 0:
            early = [held[wrap(*chip)] for chip in EARLY]
            int_all, *parts = lax.optimization_barrier([int_all, *parts, *early])[: 1 + len(parts)]
        parts = [pltpu.with_memory_space_constraint(*both) for both in zip(parts, [pltpu.VMEM, pltpu.HBM])]
        both = pltpu.HBM((CORES * occ, panel, size), f32)
        whole = pl.pallas_call(
            functools.partial(product_kernel, (occ, panel, width)),
            out_shape=both,
            in_specs=[ANY, VMEM, ANY],
            out_specs=ANY,
            scratch_shapes=[
                pltpu.VMEM(wide.shape, bf16),
                pltpu.VMEM((CORES * DEPTH, occ, panel, width), f32),
                pltpu.VMEM((CORES * height, DEPTH * width), bf16),
                pltpu.VMEM((CORES * height, DEPTH * width), bf16),
                pltpu.VMEM(both.shape, f32),
                pltpu.SemaphoreType.DMA,
                pltpu.SemaphoreType.DMA((CORES * DEPTH,)),
                pltpu.SemaphoreType.DMA((CORES * height // BLOCK,)),
            ],
            compiler_params=pltpu.CompilerParams(vmem_limit_bytes=24 * 2**20),
            cost_estimate=COSTS[n],
            name=f"product_{n}",
        )(pltpu.with_memory_space_constraint(int_all, pltpu.HBM), *parts)
        sent = lax.optimization_barrier([whole, arrays[-1][2]])[0] if arrays else whole
        swapped = lax.ppermute(whole, "core", [(0, 1), (1, 0)])
        mirror = lax.all_to_all(sent, ("core", "virt"), split_axis=0, concat_axis=0, tiled=True)
        arrays.append([whole, swapped, mirror])
        places_of.append((starts[n], size))
        if n == 0:
            int_all = lax.optimization_barrier([int_all, whole])[0]
            bring(LAST, [whole])
    fixed = lambda array, place: array if place is None else pltpu.with_memory_space_constraint(array, place)
    where = [[pltpu.HBM, pltpu.HBM, pltpu.VMEM], [pltpu.HBM, pltpu.HBM, None]]
    arrays = [[fixed(*both) for both in zip(*groups)] for groups in zip(arrays, where)]

    slots = [(chip, e) for e in range(CORES) for chips in sets for chip in chips]
    pair = (index[1] * SIDE + index[2]) * CORES + index[3]
    e_b = lax.dynamic_slice(e_vir, (pair * panel,), (panel,)).reshape(panel, 1)
    out = pl.pallas_call(
        functools.partial(finish_kernel, (occ, panel, virtuals), places_of, slots),
        out_shape=jax.ShapeDtypeStruct((occ, panel, virtuals), f32),
        in_specs=[SMEM, SMEM, SMEM, VMEM, VMEM] + [ANY, ANY, VMEM, ANY, ANY, ANY],
        out_specs=ANY,
        scratch_shapes=[
            pltpu.SMEM((virtuals // panel,), jnp.int32),
            pltpu.VMEM((occ, panel, virtuals), f32),
            pltpu.VMEM((occ, panel, virtuals), f32),
            pltpu.VMEM((occ, panel, virtuals), f32),
            pltpu.SemaphoreType.DMA((occ, 2 * CORES * len(sets))),
            pltpu.SemaphoreType.DMA((occ,)),
        ],
        compiler_params=pltpu.CompilerParams(vmem_limit_bytes=16 * 2**20),
        name="finish",
    )(places, panel_of, e_occ, e_b, e_vir.reshape(1, virtuals), *[a for group in arrays for a in group])
    return out[None]


def solution(mesh):
    fine = Mesh(mesh.devices.reshape(SIDE, SIDE, CORES, DEPTH), ("x", "y", "core", "virt"))
    rows = ("x", "y", "core")
    in_specs = (P(None, rows, "virt"), P(None, rows, "virt"), P(), P(), P())
    out_specs = P("virt", None, rows, None)
    return jax.shard_map(body, mesh=fine, in_specs=in_specs, out_specs=out_specs, check_vma=False)
```

```python
import functools

import jax
import jax.numpy as jnp
from jax import lax
from jax.experimental import pallas as pl
from jax.experimental.pallas import tpu as pltpu
from jax.sharding import Mesh, PartitionSpec as P

SIDE = 4
CORES = 2
DEPTH = 8
BLOCK = 256
NT = (((1,), (1,)), ((), ()))
SMEM = pl.BlockSpec(memory_space=pltpu.SMEM)
ANY = pl.BlockSpec(memory_space=pl.ANY)
VMEM = pl.BlockSpec(memory_space=pltpu.VMEM)
COSTS = [pl.CostEstimate(flops=f * 10**9, transcendentals=0, bytes_accessed=f * 10**6) for f in (60, 8)]
FIRST = [
    ((1, 0), (1, 0)),
    ((-1, 0), (-1, 0)),
    ((0, 1), (0, 1)),
    ((0, -1), (0, -1)),
    ((1, 1), (1, 0)),
    ((-1, -1), (-1, 0)),
    ((-1, 1), (0, 1)),
    ((1, -1), (0, -1)),
    ((2, 0), (1, 0)),
    ((0, 2), (0, 1)),
    ((2, 1), (-1, 0)),
    ((1, 2), (0, -1)),
    ((2, -1), (1, 0)),
]
LAST = [((-1, 2), (0, -1)), ((2, 2), (0, 1))]
SETS = [
    [(0, 0), (1, 0), (-1, 0), (0, 1), (0, -1), (1, 1), (-1, -1), (-1, 1)],
    [(1, -1), (2, 0), (0, 2), (2, 1), (1, 2), (2, -1), (-1, 2), (2, 2)],
]
EARLY = [(1, -1), (2, 0)]


def wrap(x, y):
    return x % SIDE, y % SIDE


def split(x):
    high = x.astype(jnp.bfloat16)
    return high, (x - high.astype(jnp.float32)).astype(jnp.bfloat16)


def split_kernel(dims, *refs):
    panel, width, chips = dims
    amps_hbm = refs[:chips]
    a_hi, a_lo_hbm, amps, a_lo, amp_sem, out_sem = refs[chips:]
    loads = [pltpu.make_async_copy(amps_hbm[g], amps.at[g], amp_sem.at[g]) for g in range(chips)]
    for copy in loads:
        copy.start()
    for g in range(chips):
        loads[g].wait()
        rows = slice(g * panel, (g + 1) * panel)
        for s in range(DEPTH):
            cols = slice(s * width, (s + 1) * width)
            a_hi[rows, cols], a_lo[rows, cols] = split(amps[g, s])
    store = pltpu.make_async_copy(a_lo, a_lo_hbm, out_sem)
    store.start()
    store.wait()


def product_kernel(dims, ints_hbm, a_hi, a_lo_hbm, whole, a_lo, ints, i_hi, i_lo, out, a_sem, int_sem, out_sem):
    occ, panel, width = dims
    loads = [pltpu.make_async_copy(ints_hbm.at[s], ints.at[s], int_sem.at[s]) for s in range(CORES * DEPTH)]
    low = pltpu.make_async_copy(a_lo_hbm, a_lo, a_sem)
    for copy in loads[:DEPTH] + [low] + loads[DEPTH:]:
        copy.start()
    height = occ * panel
    blocks = height // BLOCK
    dot = functools.partial(lax.dot_general, dimension_numbers=NT, preferred_element_type=jnp.float32)

    def cut(c, s):
        rows, cols = slice(c * height, (c + 1) * height), slice(s * width, (s + 1) * width)
        i_hi[rows, cols], i_lo[rows, cols] = split(ints[c * DEPTH + s].reshape(height, width))

    for s in range(DEPTH):
        loads[s].wait()
        cut(0, s)
    for copy in [low] + loads[DEPTH:]:
        copy.wait()
    stores = []
    for c in range(CORES):
        for m in range(blocks):
            at = slice(c * height + m * BLOCK, c * height + (m + 1) * BLOCK)
            sums = dot(i_hi[at], a_lo[...]) + dot(i_lo[at], a_hi[...]) + dot(i_hi[at], a_hi[...])
            at = slice(at.start // panel, at.stop // panel)
            out[at] = sums.reshape(BLOCK // panel, panel, -1)
            stores.append(pltpu.make_async_copy(out.at[at], whole.at[at], out_sem.at[len(stores)]))
            stores[-1].start()
            for s in range(m * DEPTH // blocks, (m + 1) * DEPTH // blocks) if c == 0 else []:
                cut(1, s)
    for copy in stores:
        copy.wait()


def finish_kernel(dims, pieces, slots, places, panel_of, e_occ, e_b, e_vir, *refs):
    occ, panel, virtuals = dims
    out_hbm, slot_of, dir_v, mir_v, out_v, in_sem, out_sem = refs[3 * len(pieces) :]
    v, x, y, core = places[0], places[1], places[2], places[3]
    loads = []
    for j in range(occ):
        mine = []
        for n, (first, size) in enumerate(pieces):
            own, other, mirror = refs[3 * n : 3 * n + 3]
            for e in range(CORES):
                at = (j, slice(None), pl.ds(e * virtuals // 2 + first, size))
                mine.append(((other if e else own).at[core * occ + j], dir_v.at[at]))
                mine.append((mirror.at[lax.rem(core + e, CORES) * occ + j], mir_v.at[at]))
        loads.append([pltpu.make_async_copy(a, b, in_sem.at[j, n]) for n, (a, b) in enumerate(mine)])
        for copy in loads[j]:
            copy.start()
    for s, ((dx, dy), e) in enumerate(slots):
        chip = lax.rem(x + dx, SIDE) * SIDE + lax.rem(y + dy, SIDE)
        slot_of[panel_of[chip * CORES + lax.rem(core + e, CORES)]] = s
    lanes = 2 * panel
    lane = lax.broadcasted_iota(jnp.int32, (panel, lanes), 1)
    for j in range(occ):
        for copy in loads[j]:
            copy.wait()
        base = (e_occ[v] + e_occ[j]) - e_b[...]
        for t in range(virtuals // lanes):
            sides = []
            for h in range(2):
                s = slot_of[2 * t + h]
                cols = pl.ds(pl.multiple_of((s // 2) * lanes, lanes), lanes)
                diff = dir_v[j, :, cols] - mir_v[j, :, cols]
                sides.append(pltpu.roll(diff, lax.rem(s + h, 2) * panel, 1))
            cols = slice(t * lanes, (t + 1) * lanes)
            out_v[j, :, cols] = jnp.where(lane < panel, sides[0], sides[1]) / (base - e_vir[:, cols])
        pltpu.make_async_copy(out_v.at[j], out_hbm.at[j], out_sem.at[j]).start()
    for j in range(occ):
        pltpu.make_async_copy(out_v.at[j], out_hbm.at[j], out_sem.at[j]).wait()


def body(amps, ints, panel_of, e_occ, e_vir):
    occ, panel, width = amps.shape
    virtuals = e_vir.shape[0]
    f32, bf16 = jnp.float32, jnp.bfloat16
    index = [lax.axis_index(name).astype(jnp.int32) for name in ("virt", "x", "y", "core")]
    places = jnp.stack(index)

    def move(data, dx, dy):
        name, step = ("x", dx) if dx else ("y", dy)
        return lax.ppermute(data, name, [(n, (n - step) % SIDE) for n in range(SIDE)])

    int_all = lax.all_gather(ints, ("core", "virt"), axis=0)
    held = {(0, 0): lax.all_to_all(amps, "virt", split_axis=0, concat_axis=0, tiled=True)}
    sets = [[wrap(*chip) for chip in chips] for chips in SETS]
    starts = [sum(map(len, sets[:k])) * panel for k in range(len(sets))]

    def bring(routes, after=()):
        for to, (dx, dy) in routes:
            data = held[wrap(to[0] - dx, to[1] - dy)]
            if after:
                data = lax.optimization_barrier([data, *after])[0]
            held[wrap(*to)] = move(data, dx, dy)

    bring(FIRST)
    arrays, places_of = [], []
    for n, chips in enumerate(sets):
        size = len(chips) * panel
        height = occ * panel
        wide = jax.ShapeDtypeStruct((size, DEPTH * width), bf16)
        parts = pl.pallas_call(
            functools.partial(split_kernel, (panel, width, len(chips))),
            out_shape=[wide, pltpu.HBM(wide.shape, bf16)],
            in_specs=[ANY] * len(chips),
            out_specs=[VMEM, ANY],
            scratch_shapes=[
                pltpu.VMEM((len(chips), DEPTH, panel, width), f32),
                pltpu.VMEM(wide.shape, bf16),
                pltpu.SemaphoreType.DMA((len(chips),)),
                pltpu.SemaphoreType.DMA,
            ],
            compiler_params=pltpu.CompilerParams(vmem_limit_bytes=8 * 2**20),
            cost_estimate=COSTS[n],
            name=f"split_{n}",
        )(*[pltpu.with_memory_space_constraint(held[chip], pltpu.HBM) for chip in chips])
        if n == 0:
            early = [held[wrap(*chip)] for chip in EARLY]
            int_all, *parts = lax.optimization_barrier([int_all, *parts, *early])[: 1 + len(parts)]
        parts = [pltpu.with_memory_space_constraint(*both) for both in zip(parts, [pltpu.VMEM, pltpu.HBM])]
        both = pltpu.HBM((CORES * occ, panel, size), f32)
        whole = pl.pallas_call(
            functools.partial(product_kernel, (occ, panel, width)),
            out_shape=both,
            in_specs=[ANY, VMEM, ANY],
            out_specs=ANY,
            scratch_shapes=[
                pltpu.VMEM(wide.shape, bf16),
                pltpu.VMEM((CORES * DEPTH, occ, panel, width), f32),
                pltpu.VMEM((CORES * height, DEPTH * width), bf16),
                pltpu.VMEM((CORES * height, DEPTH * width), bf16),
                pltpu.VMEM(both.shape, f32),
                pltpu.SemaphoreType.DMA,
                pltpu.SemaphoreType.DMA((CORES * DEPTH,)),
                pltpu.SemaphoreType.DMA((CORES * height // BLOCK,)),
            ],
            compiler_params=pltpu.CompilerParams(vmem_limit_bytes=24 * 2**20),
            cost_estimate=COSTS[n],
            name=f"product_{n}",
        )(pltpu.with_memory_space_constraint(int_all, pltpu.HBM), *parts)
        sent = lax.optimization_barrier([whole, arrays[-1][2]])[0] if arrays else whole
        swapped = lax.ppermute(whole, "core", [(0, 1), (1, 0)])
        mirror = lax.all_to_all(sent, ("core", "virt"), split_axis=0, concat_axis=0, tiled=True)
        arrays.append([whole, swapped, mirror])
        places_of.append((starts[n], size))
        if n == 0:
            int_all = lax.optimization_barrier([int_all, whole])[0]
            bring(LAST, [whole])
    fixed = lambda array, place: array if place is None else pltpu.with_memory_space_constraint(array, place)
    where = [[pltpu.HBM, pltpu.HBM, pltpu.VMEM], [pltpu.HBM, pltpu.HBM, None]]
    arrays = [[fixed(*both) for both in zip(*groups)] for groups in zip(arrays, where)]

    slots = [(chip, e) for e in range(CORES) for chips in sets for chip in chips]
    pair = (index[1] * SIDE + index[2]) * CORES + index[3]
    e_b = lax.dynamic_slice(e_vir, (pair * panel,), (panel,)).reshape(panel, 1)
    out = pl.pallas_call(
        functools.partial(finish_kernel, (occ, panel, virtuals), places_of, slots),
        out_shape=jax.ShapeDtypeStruct((occ, panel, virtuals), f32),
        in_specs=[SMEM, SMEM, SMEM, VMEM, VMEM] + [ANY, ANY, VMEM, ANY, ANY, ANY],
        out_specs=ANY,
        scratch_shapes=[
            pltpu.SMEM((virtuals // panel,), jnp.int32),
            pltpu.VMEM((occ, panel, virtuals), f32),
            pltpu.VMEM((occ, panel, virtuals), f32),
            pltpu.VMEM((occ, panel, virtuals), f32),
            pltpu.SemaphoreType.DMA((occ, 2 * CORES * len(sets))),
            pltpu.SemaphoreType.DMA((occ,)),
        ],
        compiler_params=pltpu.CompilerParams(vmem_limit_bytes=16 * 2**20),
        name="finish",
    )(places, panel_of, e_occ, e_b, e_vir.reshape(1, virtuals), *[a for group in arrays for a in group])
    return out[None]


def solution(mesh):
    fine = Mesh(mesh.devices.reshape(SIDE, SIDE, CORES, DEPTH), ("x", "y", "core", "virt"))
    rows = ("x", "y", "core")
    in_specs = (P(None, rows, "virt"), P(None, rows, "virt"), P(), P(), P())
    out_specs = P("virt", None, rows, None)
    return jax.shard_map(body, mesh=fine, in_specs=in_specs, out_specs=out_specs, check_vma=False)
```
